256 devices in a mesh: section: 4 (over y_hi, core), expert: 64 (over x, y_lo, z).
Axes of the slice: x: 4, y: 4 (y_hi: 2, y_lo: 2; y = y_hi * 2 + y_lo), z: 8, core: 2. Of those that a mesh axis runs over, the one named last changes fastest.
Arguments:
- pending_groups: bfloat16 [4, 8192, 2048], P('section', 'expert'), may hold values from -6 to 6
- stratum_rescale_factors: float32 [4, 2048], P('section'), may hold values from 0.1 to 1.9
- ending_rescale_factor: float32 [2048], replicated, may hold values from 0.1 to 1.9
- assigned_specialists: int32 [4, 8192, 8], P('section', 'expert'), may hold values from 0 to 63, all different within a row; in each aligned block of 128 rows (0 to 127, 128 to 255, ..., all dimensions but the last counted through in order) at most 24 rows name the same one
- mixing_factors: float32 [4, 8192, 8], P('section', 'expert'), may hold values from 0.1 to 0.7
- specialist_raising_matrix: bfloat16 [4, 64, 2048, 1536], P('section', 'expert'), may hold values from -0.125 to 0.125
- specialist_lowering_matrix: bfloat16 [4, 64, 768, 2048], P('section', 'expert'), may hold values from -0.21875 to 0.21875
Outputs:
- arrived: bfloat16 [4, 8192, 2048], P('section', 'expert')
The draws below stay inside these ranges and needn't reach their ends.
Inputs may be any that keep to these rules, and one draw needn't show every extreme that they name: `assigned_specialists`: within each aligned block of 128 tokens of one section (the tokens of one device), every expert is named by at most 24 tokens, a bound that some block reaches.
All inputs are finite; a program needn't handle non-finite values. Where the reference program divides by a largest or mean magnitude, that divisor is 1e-20 or more.
Results may differ from the reference program's by a relative error of at most 0.0062.
Values may be sent and summed in bfloat16 or wider, within the bound.
A program may use at most 128 MiB of HBM per device.

```python
import math
import jax
import jax.numpy as jnp
import numpy as np
from jax import lax

HIDDEN_EXTENT = 2048
FFE = 768
TOP = 8
BLOCK = 128
TOK_DEV = 128
CHAIN_LINKS = 4
EXPERTS = 64
GROUP_ITEMS = 8192
CAP = 24
N_EXPERT = 64


def levels(key, shape, pieces, smallest, top_value):
    factor_of = 1.0
    for axis_at, shards_of in pieces:
        heights = jax.random.uniform(jax.random.fold_in(jax.random.fold_in(key, 6), axis_at), (shards_of,), jnp.float32, smallest / len(pieces), top_value / len(pieces))
        factor_of = factor_of * jnp.repeat(jnp.exp(heights), shape[axis_at] // shards_of).reshape((-1,) + (1,) * (len(shape) - 1 - axis_at))
    return factor_of


def routed_block(stream_key, own, number, rows, number_of, top, reach, skew):
    sequence = jax.random.permutation(stream_key, number_of)
    crowded, usual = shares(number_of, rows * top, reach, skew, True), shares(number_of, rows * top, reach, skew, False)
    places = jnp.arange(number_of)

    def named(tallies, turn):
        used = int((tallies > 0).sum())
        fixed = max(1, used // 4)
        shifted = fixed + (places - fixed + turn * (used - fixed)) % max(1, number_of - fixed)
        return jnp.zeros((number_of,), jnp.int32).at[sequence[jnp.where(places < fixed, places, shifted)]].set(jnp.asarray(tallies, jnp.int32))

    tallies = jnp.where(number % 4 == 0, named(crowded, number // 4), named(usual, number - number // 4 - 1))
    mixed = jax.random.permutation(jax.random.fold_in(own, 3), number_of)
    donor, taker = mixed[0:number_of // 2 * 2:2], mixed[1:number_of // 2 * 2:2]
    slack = jnp.minimum(tallies[donor] - 1, reach - tallies[taker]) // 2
    slack = jnp.where((donor == sequence[0]) | (taker == sequence[0]) | (tallies[taker] == 0), 0, jnp.maximum(slack, 0))
    shifted = jax.random.randint(jax.random.fold_in(own, 4), (number_of // 2,), 0, 1 << 20) % (slack + 1)
    tallies = tallies.at[donor].add(-shifted).at[taker].add(shifted)
    items = jnp.searchsorted(jnp.cumsum(tallies), jnp.arange(rows * top), side="right").astype(jnp.int32)
    listing = items.reshape(top, rows).T
    listing = listing[jax.random.permutation(jax.random.fold_in(own, 1), rows)]
    turn = jax.random.randint(jax.random.fold_in(own, 2), (rows, 1), 0, top)
    return jnp.take_along_axis(listing, (jnp.arange(top)[None, :] + turn) % top, axis=1)


def shares(amount, total, most, skew, full):
    portions = [(1 << 20) // math.isqrt(grade ** skew) + 1 for grade in range(1, amount + 1)]
    largest = most if full else min(most, max(-(-total // amount), total * portions[0] // sum(portions)))
    least = 1 if total - largest >= amount - 1 else 0
    counts, rest = [largest] + [least] * (amount - 1), total - largest - least * (amount - 1)
    while rest > 0:
        candidates = [i for i in range(1, amount) if counts[i] < largest] or [i for i in range(1, amount) if counts[i] < most]
        whole, remaining = sum([portions[i] for i in candidates]), rest
        for i in candidates:
            more = min(most - counts[i], max(1, remaining * portions[i] // whole), rest)
            counts[i] = counts[i] + more
            rest = rest - more
    return np.array(counts)


def noise(own_key, extent, scale, limit, shards=(), kind=jnp.bfloat16):
    values = scale * jax.random.normal(own_key, extent, jnp.float32)
    if shards:
        values = values * levels(own_key, extent, shards, -0.22, 0.18)
    return jnp.clip(values, -limit, limit).astype(kind)


def setup_inputs(seed: int = 0) -> dict:
    seeds = jax.random.split(jax.random.key(seed), 8)
    pending_groups = noise(seeds[0], (CHAIN_LINKS, GROUP_ITEMS, HIDDEN_EXTENT), 1.0, 6.0, ((0, 4), (1, 64)))
    stratum_rescale_factors = jnp.clip(1.0 + 0.18 * jax.random.normal(seeds[1], (CHAIN_LINKS, HIDDEN_EXTENT), jnp.float32), 0.1, 1.9)
    ending_rescale_factor = jnp.clip(1.0 + 0.18 * jax.random.normal(seeds[2], (HIDDEN_EXTENT,), jnp.float32), 0.1, 1.9)
    assigned_specialists_keys = jax.random.split(jax.random.fold_in(seeds[3], 1), CHAIN_LINKS * GROUP_ITEMS // TOK_DEV)
    assigned_specialists_turns = jax.random.permutation(jax.random.fold_in(seeds[3], 3), CHAIN_LINKS * GROUP_ITEMS // TOK_DEV)
    assigned_specialists = jax.vmap(lambda own, number: routed_block(jax.random.fold_in(seeds[3], 2), own, number, TOK_DEV, EXPERTS, TOP, CAP, 1))(assigned_specialists_keys, assigned_specialists_turns).reshape((CHAIN_LINKS, GROUP_ITEMS, TOP))
    mixing_factors = jnp.clip(0.1 + 0.59999999 * jax.random.uniform(seeds[4], (CHAIN_LINKS, GROUP_ITEMS, TOP), jnp.float32) ** levels(seeds[4], (CHAIN_LINKS, GROUP_ITEMS, TOP), ((0, 4), (1, 64)), -0.2, 0.2), 0.1, 0.7)
    specialist_raising_matrix = noise(seeds[5], (CHAIN_LINKS, EXPERTS, HIDDEN_EXTENT, 2 * FFE), HIDDEN_EXTENT ** -0.5, 0.125, ((0, 4), (1, 64)))
    specialist_lowering_matrix = noise(seeds[6], (CHAIN_LINKS, EXPERTS, FFE, HIDDEN_EXTENT), FFE ** -0.5, 0.21875, ((0, 4), (1, 64)))
    return {"pending_groups": pending_groups, "stratum_rescale_factors": stratum_rescale_factors, "ending_rescale_factor": ending_rescale_factor, "assigned_specialists": assigned_specialists, "mixing_factors": mixing_factors, "specialist_raising_matrix": specialist_raising_matrix, "specialist_lowering_matrix": specialist_lowering_matrix}


EPS = 1e-06

def rms_scale(values, norm_gain):
    widened = values.astype(jnp.float32)
    return widened * lax.rsqrt(lax.optimization_barrier(jnp.mean(widened * widened, axis=-1, keepdims=True)) + EPS) * norm_gain

def restore_rows(normed):
    lead_count = normed.shape[0]
    blocks = normed.reshape(lead_count, -1, BLOCK)
    scales = (lax.optimization_barrier(jnp.max(jnp.abs(blocks), axis=-1, keepdims=True)) + EPS).astype(jnp.bfloat16)
    quantized = lax.optimization_barrier((blocks / scales.astype(jnp.float32)).astype(jnp.bfloat16))
    restored = quantized.astype(jnp.float32) * scales.astype(jnp.float32)
    return restored.astype(jnp.bfloat16).reshape(lead_count, -1)

def specialist_mixture_apply(item_group, norm_gain, routing, weights, gate_up, down):
    restored = restore_rows(rms_scale(item_group, norm_gain))
    most_rows = N_EXPERT * CAP

    def add_expert(expert, running):
        selected = routing == expert
        weight = lax.optimization_barrier(jnp.sum(jnp.where(selected, weights, 0.0), axis=1))
        chosen = jnp.any(selected, axis=1)
        picked_rows = jnp.nonzero(chosen, size=most_rows, fill_value=0)[0]
        rows = restored[picked_rows]
        gate_and_up = jnp.dot(rows, gate_up[expert], preferred_element_type=jnp.float32)
        hidden = (jax.nn.silu(gate_and_up[:, :FFE]) * gate_and_up[:, FFE:]).astype(jnp.bfloat16)
        out_rows = jnp.dot(hidden, down[expert], preferred_element_type=jnp.float32).astype(jnp.bfloat16)
        in_range = jnp.arange(most_rows) < jnp.sum(chosen.astype(jnp.int32))
        scaled = jnp.where(in_range[:, None], weight[picked_rows][:, None] * out_rows.astype(jnp.float32), 0.0)
        return running.at[picked_rows].add(scaled)
    running = lax.fori_loop(0, EXPERTS, add_expert, jnp.zeros(item_group.shape, jnp.float32))
    return (item_group.astype(jnp.float32) + running).astype(jnp.bfloat16)

def reference(pending_groups, stratum_rescale_factors, ending_rescale_factor, assigned_specialists, mixing_factors, specialist_raising_matrix, specialist_lowering_matrix):
    stratum_results = [specialist_mixture_apply(pending_groups[chain_link_apply], stratum_rescale_factors[chain_link_apply], assigned_specialists[chain_link_apply], mixing_factors[chain_link_apply], specialist_raising_matrix[chain_link_apply], specialist_lowering_matrix[chain_link_apply]) for chain_link_apply in range(CHAIN_LINKS)]
    normed_last = rms_scale(stratum_results[-1], ending_rescale_factor).astype(jnp.bfloat16)
    return jnp.stack([normed_last] + stratum_results[:-1])
```

```python
import jax
import jax.numpy as jnp
from jax import lax
from jax.sharding import PartitionSpec as P

BLOCK = 128
EPS = 1e-06
NZ = 8
CAPACITY = 24


def rms_scale(values, norm_gain):
    widened = values.astype(jnp.float32)
    return (
        widened * lax.rsqrt(jnp.mean(widened * widened, axis=-1, keepdims=True) + EPS) * norm_gain
    )


def restore_rows(normed):
    blocks = normed.reshape(normed.shape[0], -1, BLOCK)
    scales = (jnp.max(jnp.abs(blocks), axis=-1, keepdims=True) + EPS).astype(jnp.bfloat16)
    scales = scales.astype(jnp.float32)
    quantized = (blocks / scales).astype(jnp.bfloat16)
    restored = quantized.astype(jnp.float32) * scales
    return restored.astype(jnp.bfloat16).reshape(normed.shape)


def local(pending, gain, final_gain, assigned, mixing, raising, lowering):
    item_group = pending[0]
    routing = assigned[0]
    weight = mixing[0]
    gate_up = raising[0, 0]
    down = lowering[0, 0]
    owners = lax.axis_size("expert")
    planes = NZ
    columns = owners // planes
    tok_count, top = routing.shape
    width = item_group.shape[1]
    hidden_width = down.shape[0]
    line_groups = [[c * planes + z for z in range(planes)] for c in range(columns)]
    plane_groups = [[c * planes + z for c in range(columns)] for z in range(planes)]
    plane = lax.axis_index("expert") % planes

    chosen = routing[:, :, None] == jnp.arange(owners, dtype=jnp.int32)
    named = jnp.any(chosen, axis=1)
    share = jnp.sum(jnp.where(chosen, weight[:, :, None], 0.0), axis=1)
    earlier = jnp.tril(jnp.ones((tok_count, tok_count), jnp.bfloat16), -1)
    slot = jnp.dot(earlier, named.astype(jnp.bfloat16), preferred_element_type=jnp.float32)
    slot = jnp.where(named, slot, -1.0)
    restored = restore_rows(rms_scale(item_group, gain[0]))
    packet = jnp.concatenate(
        [restored, slot.astype(jnp.bfloat16), share.astype(jnp.bfloat16)], axis=1
    )
    line = lax.all_gather(packet, "expert", axis_index_groups=line_groups)

    def of_plane(part):
        return lax.dynamic_index_in_dim(
            part.reshape(planes, tok_count, columns, planes), plane, 3, keepdims=False
        )

    slots = of_plane(line[:, :, width : width + owners])
    shares = of_plane(line[:, :, width + owners :])
    match = slots[..., None] == jnp.arange(CAPACITY, dtype=jnp.bfloat16)
    pick = match.astype(jnp.bfloat16)
    mix = jnp.where(match, shares[..., None], 0)
    rows = jnp.einsum(
        "btjc,bth->jbch", pick, line[:, :, :width], preferred_element_type=jnp.float32
    ).astype(jnp.bfloat16)
    rows = lax.all_to_all(
        rows, "expert", split_axis=0, concat_axis=0, tiled=True, axis_index_groups=plane_groups
    ).reshape(-1, width)
    both = jnp.dot(rows, gate_up, preferred_element_type=jnp.float32)
    hidden = (jax.nn.silu(both[:, :hidden_width]) * both[:, hidden_width:]).astype(jnp.bfloat16)
    result = jnp.dot(hidden, down, preferred_element_type=jnp.float32).astype(jnp.bfloat16)
    result = lax.all_to_all(
        result.reshape(columns, planes, CAPACITY, width),
        "expert",
        split_axis=0,
        concat_axis=0,
        tiled=True,
        axis_index_groups=plane_groups,
    )
    partial = jnp.einsum(
        "btjc,jbch->bth", mix, result, preferred_element_type=jnp.float32
    ).astype(jnp.bfloat16)
    partial = partial.reshape(planes * tok_count, width)
    mixture = lax.psum_scatter(
        partial, "expert", scatter_dimension=0, axis_index_groups=line_groups, tiled=True
    )
    layer_out = (item_group.astype(jnp.float32) + mixture.astype(jnp.float32)).astype(jnp.bfloat16)
    sections = lax.axis_size("section")
    arriving = lax.ppermute(
        layer_out, "section", [(i, (i + 1) % sections) for i in range(sections)]
    )
    arrived = jnp.where(
        lax.axis_index("section") == 0,
        rms_scale(arriving, final_gain).astype(jnp.bfloat16),
        arriving,
    )
    return arrived[None]


def solution(mesh):
    in_specs = (
        P("section", "expert", None),
        P("section", None),
        P(),
        P("section", "expert", None),
        P("section", "expert", None),
        P("section", "expert", None, None),
        P("section", "expert", None, None),
    )
    out_specs = P("section", "expert", None)
    return jax.shard_map(local, mesh=mesh, in_specs=in_specs, out_specs=out_specs, check_vma=False)
```

```python
import functools

import jax
import jax.numpy as jnp
from jax import lax
from jax.experimental import pallas as pl
from jax.experimental.pallas import tpu as pltpu
from jax.sharding import PartitionSpec as P

MESH = pl.DeviceIdType.MESH
F32, BF16 = jnp.float32, jnp.bfloat16
BLOCK = 128
EPS = 1e-06
NX, NY, NZ = 4, 2, 8
PLANE = NX * NY
FAR = NZ // 2
CAPACITY = 24
PAIR = 2 * CAPACITY
ROWS = PLANE * PAIR
PARTS = 2
TILE = 256
LANES = 128


def dot(a, b):
    return jnp.dot(a, b, preferred_element_type=F32)


def dot_nt(a, b):
    return lax.dot_general(a, b, (((1,), (1,)), ((), ())), preferred_element_type=F32)


def body(
    x_ref, gain_ref, final_ref, route_ref, mixing_ref, up_ref, down_ref, out_ref,
    line, meta, srow, rrow, orow, ret, mix, pick, spread, spread_t, wup, wdown, hid,
    acc, rsout, rsin, layer, arrive,
    ag_send, ag_recv, am_send, am_recv, d_send, d_recv, r_send, r_recv,
    rs_send, rs_recv, sec_send, sec_recv, w_sem,
):
    tokens, width = x_ref.shape
    part = width // PARTS
    hidden = wdown.shape[0]
    top = route_ref.shape[1]
    per_part = part // BLOCK
    tiles = part // TILE
    experts = PLANE * NZ
    half = tokens // 2
    me = lax.axis_index("expert")
    section = lax.axis_index("section")
    sections = lax.axis_size("section")
    mx, my, mz = me // (NY * NZ), (me // NZ) % NY, me % NZ

    def in_plane(sign, offset):
        dx, dy = offset // NY, offset % NY
        return (((mx + sign * dx + NX) % NX) * NY + (my + dy) % NY) * NZ + mz

    column = me - mz
    around = (column + (mz + 1) % NZ, column + (mz + NZ - 1) % NZ)
    following = (section + 1) % sections
    previous = (section + sections - 1) % sections

    weights = [
        pltpu.make_async_copy(up_ref, wup, w_sem.at[0]),
        pltpu.make_async_copy(down_ref, wdown, w_sem.at[1]),
    ]
    for copy in weights:
        copy.start()

    barrier = pltpu.get_barrier_semaphore()

    def greet(offset, carry):
        pl.semaphore_signal(
            barrier, 1, device_id={"expert": in_plane(1, offset)}, device_id_type=MESH
        )
        return carry

    lax.fori_loop(1, PLANE, greet, 0)
    for peer in around:
        pl.semaphore_signal(barrier, 1, device_id={"expert": peer}, device_id_type=MESH)
    for peer in (following, previous):
        pl.semaphore_signal(barrier, 1, device_id={"section": peer}, device_id_type=MESH)

    squares = jnp.zeros((tokens, BLOCK), F32)
    for b in range(width // BLOCK):
        values = x_ref[:, b * BLOCK : (b + 1) * BLOCK].astype(F32)
        squares = squares + values * values
    inverse = lax.rsqrt(jnp.sum(squares, axis=1, keepdims=True) / width + EPS)

    def restore(b, carry):
        cols = pl.ds(pl.multiple_of(b * BLOCK, BLOCK), BLOCK)
        normed = x_ref[:, cols].astype(F32) * inverse * gain_ref[:, cols]
        scale = jnp.max(jnp.abs(normed), axis=1, keepdims=True) + EPS
        scale = scale.astype(BF16).astype(F32)
        quantized = (normed / scale).astype(BF16).astype(F32)
        place = pl.ds(pl.multiple_of((b % per_part) * BLOCK, BLOCK), BLOCK)
        line[b // per_part, 0, :, place] = (quantized * scale).astype(BF16)
        return carry

    lax.fori_loop(0, width // BLOCK, restore, 0)

    lane = lax.broadcasted_iota(jnp.int32, (tokens, LANES), 1)
    named = jnp.zeros((tokens, LANES), F32)
    share = jnp.zeros((tokens, LANES), F32)
    for k in range(top):
        name = route_ref[:, k : k + 1]
        named = named + jnp.where(lane == name, 1.0, 0.0)
        share = share + jnp.where(lane - experts == name, mixing_ref[:, k : k + 1], 0.0)
    up_to = lax.broadcasted_iota(jnp.int32, (tokens, tokens), 0)
    up_to = up_to >= lax.broadcasted_iota(jnp.int32, (tokens, tokens), 1)
    place = dot(jnp.where(up_to, 1.0, 0.0).astype(BF16), named.astype(BF16))
    meta[0] = jnp.where(lane < experts, place * named, share).astype(BF16)

    def slots(shape, dim):
        q = lax.broadcasted_iota(jnp.int32, shape, dim)
        offset = jnp.zeros(shape, jnp.int32)
        for i in range(1, PLANE):
            offset = offset + jnp.where(q >= i * PAIR, 1, 0)
        q = q - offset * PAIR
        second = jnp.where(q >= CAPACITY, 1, 0)
        return offset, second, q - second * CAPACITY

    def owner(offset):
        dx, dy = offset // NY if isinstance(offset, int) else offset >> 1, offset & 1
        return ((((mx + dx) & (NX - 1)) * NY) + ((my + dy) & (NY - 1))) * NZ + mz

    offset, second, _ = slots((LANES, ROWS), 1)
    expert = owner(offset)
    lane_of = lax.broadcasted_iota(jnp.int32, (LANES, ROWS), 0)
    for i in range(2):
        for j in range(2):
            hit = (lane_of == expert + j * experts) & (second == i)
            spread[2 * j + i] = jnp.where(hit, 1.0, 0.0).astype(BF16)
    offset, second, _ = slots((ROWS, LANES), 0)
    expert = owner(offset)
    lane_of = lax.broadcasted_iota(jnp.int32, (ROWS, LANES), 1)
    for i in range(2):
        hit = (lane_of == expert) & (second == i)
        spread_t[i] = jnp.where(hit, 1.0, 0.0).astype(BF16)

    def few(step, direction):
        if step < FAR - 1:
            return pl.ds(0, tokens)
        return pl.ds(direction * half, half)

    def gather(direction, step, h):
        source, target = ((NZ - step) % NZ, NZ - 1 - step) if direction == 0 else (step, step + 1)
        rows = few(step, direction)
        return pltpu.make_async_remote_copy(
            line.at[h, source, rows], line.at[h, target, rows],
            ag_send.at[direction, step, h], ag_recv.at[direction, step, h],
            device_id={"expert": around[direction]}, device_id_type=MESH,
        )

    def gather_meta(direction, step):
        source, target = ((NZ - step) % NZ, NZ - 1 - step) if direction == 0 else (step, step + 1)
        rows = few(step, direction)
        return pltpu.make_async_remote_copy(
            meta.at[source, rows], meta.at[target, rows],
            am_send.at[direction, step], am_recv.at[direction, step],
            device_id={"expert": around[direction]}, device_id_type=MESH,
        )

    def build(c, first, last):
        _, _, want = slots((ROWS, tokens), 0)
        want = (want + 1).astype(F32)
        for i, rel in enumerate((first, last)):
            found = dot_nt(spread_t[i], meta[rel])
            pick[:, i * tokens : (i + 1) * tokens] = jnp.where(found == want, 1.0, 0.0).astype(BF16)
        _, _, want = slots((tokens, ROWS), 1)
        want = (want + 1).astype(F32)
        for i, rel in enumerate((first, last)):
            found = dot(meta[rel], spread[i])
            weight = dot(meta[rel], spread[2 + i])
            mix[c, i * tokens : (i + 1) * tokens] = jnp.where(found == want, weight, 0.0).astype(BF16)

    def select(c, first, last, h):
        def tile(n, carry):
            cols = pl.ds(pl.multiple_of(n * TILE, TILE), TILE)
            both = jnp.concatenate([line[h, first, :, cols], line[h, last, :, cols]], axis=0)
            rows = dot(pick[...], both).astype(BF16)
            srow[h, c, :, cols] = rows
            rrow[h, c, pl.ds(0, PAIR), cols] = rows[:PAIR]
            return carry

        lax.fori_loop(0, tiles, tile, 0)

    def plane_copy(source, target, send, recv, sign, offset, c, h):
        rows = pl.ds(pl.multiple_of(offset * PAIR, 16), PAIR)
        return pltpu.make_async_remote_copy(
            source.at[h, c, rows], target.at[h, c, rows], send.at[c, h], recv.at[c, h],
            device_id={"expert": in_plane(sign, offset)}, device_id_type=MESH,
        )

    def plane_all(source, target, send, recv, c, h):
        rows = pl.ds(PAIR, ROWS - PAIR)
        return pltpu.make_async_remote_copy(
            source.at[h, c, rows], target.at[h, c, rows], send.at[c, h], recv.at[c, h],
            device_id={"expert": in_plane(1, 1)}, device_id_type=MESH,
        )

    def dispatch(c, h):
        def send(offset, carry):
            plane_copy(srow, rrow, d_send, d_recv, 1, offset, c, h).start()
            return carry

        lax.fori_loop(1, PLANE, send, 0)

    def give_back(c, h):
        def send(offset, carry):
            plane_copy(orow, ret, r_send, r_recv, -1, offset, c, h).start()
            return carry

        lax.fori_loop(1, PLANE, send, 0)

    dispatched = functools.partial(plane_all, srow, rrow, d_send, d_recv)
    given_back = functools.partial(plane_all, orow, ret, r_send, r_recv)

    def expert_rows(c):
        for h in range(PARTS):
            dispatched(c, h).wait_recv()

        def gate(n, carry):
            total = []
            for base in (0, hidden):
                cols = pl.ds(pl.multiple_of(base + n * TILE, TILE), TILE)
                total.append(
                    dot(rrow[0, c], wup[pl.ds(0, part), cols])
                    + dot(rrow[1, c], wup[pl.ds(part, part), cols])
                )
            g, u = total
            cols = pl.ds(pl.multiple_of(n * TILE, TILE), TILE)
            hid[:, cols] = (g / (1.0 + jnp.exp(-g)) * u).astype(BF16)
            return carry

        lax.fori_loop(0, hidden // TILE, gate, 0)

        def lower(n, carry):
            wide = pl.ds(pl.multiple_of(n * TILE, TILE), TILE)
            cols = pl.ds(pl.multiple_of((n % tiles) * TILE, TILE), TILE)
            rows = dot(hid[...], wdown[:, wide]).astype(BF16)
            orow[n // tiles, c, :, cols] = rows
            ret[n // tiles, c, pl.ds(0, PAIR), cols] = rows[:PAIR]
            return carry

        lax.fori_loop(0, PARTS * tiles, lower, 0)

    def scatter(direction, step, h):
        source = FAR - step if direction == 0 else FAR + step
        rows = pl.ds(0, tokens) if step else pl.ds(direction * half, half)
        return pltpu.make_async_remote_copy(
            rsout.at[h, source, rows], rsin.at[h, direction, step, rows],
            rs_send.at[direction, step, h], rs_recv.at[direction, step, h],
            device_id={"expert": around[direction]}, device_id_type=MESH,
        )

    def combine(c, h):
        step = FAR - c if c else 0
        given_back(c, h).wait_recv()
        if step:
            for direction in range(2):
                scatter(direction, step - 1, h).wait_recv()

        def tile(n, carry):
            cols = pl.ds(pl.multiple_of(n * TILE, TILE), TILE)
            wide = pl.ds(pl.multiple_of(h * part + n * TILE, TILE), TILE)
            sums = dot(mix[c], ret[h, c, :, cols])
            near, away = sums[:tokens], sums[tokens:]
            if step == 0:
                acc[h, :, cols] = near + x_ref[:, wide].astype(F32)
                rsout[h, FAR, :, cols] = away.astype(BF16)
                return carry
            if step == 1:
                low, high = pl.ds(0, half), pl.ds(half, half)
                rsout[h, c, low, cols] = (near[:half] + rsin[h, 0, 0, low, cols].astype(F32)).astype(BF16)
                rsout[h, c, high, cols] = near[half:].astype(BF16)
                rsout[h, NZ - c, low, cols] = away[:half].astype(BF16)
                rsout[h, NZ - c, high, cols] = (away[half:] + rsin[h, 1, 0, high, cols].astype(F32)).astype(BF16)
                return carry
            rsout[h, c, :, cols] = (near + rsin[h, 0, step - 1, :, cols].astype(F32)).astype(BF16)
            rsout[h, NZ - c, :, cols] = (away + rsin[h, 1, step - 1, :, cols].astype(F32)).astype(BF16)
            return carry

        lax.fori_loop(0, tiles, tile, 0)
        for direction in range(2):
            scatter(direction, step, h).start()

    def onward(h):
        return pltpu.make_async_remote_copy(
            layer.at[h], arrive.at[h], sec_send.at[h], sec_recv.at[h],
            device_id={"section": following}, device_id_type=MESH,
        )

    pl.semaphore_wait(barrier, PLANE - 1 + 4)

    for direction in range(2):
        gather_meta(direction, 0).start()
    for h in range(PARTS):
        for direction in range(2):
            gather(direction, 0, h).start()
    for step in range(1, FAR + 1):
        c = step % FAR
        first, last = (step, NZ - step) if c else (0, FAR)
        for direction in range(2):
            gather_meta(direction, step - 1).wait_recv()
            if c:
                gather_meta(direction, step).start()
        build(c, first, last)
        for h in range(PARTS):
            for direction in range(2):
                gather(direction, step - 1, h).wait_recv()
                if c:
                    gather(direction, step, h).start()
            select(c, first, last, h)
            dispatch(c, h)

    for copy in weights:
        copy.wait()
    for c in range(1, FAR):
        expert_rows(c)
    for h in range(PARTS):
        give_back(FAR - 1, h)
    expert_rows(0)
    for h in range(PARTS):
        give_back(0, h)
    for c in range(FAR - 2, 0, -1):
        for h in range(PARTS):
            give_back(c, h)
    for c in (0, *range(FAR - 1, 0, -1)):
        for h in range(PARTS):
            combine(c, h)
    for h in range(PARTS):
        for direction in range(2):
            scatter(direction, FAR - 1, h).wait_recv()
        total = acc[h] + rsin[h, 0, FAR - 1].astype(F32) + rsin[h, 1, FAR - 1].astype(F32)
        layer[h] = total.astype(BF16)
        onward(h).start()
    for h in range(PARTS):
        onward(h).wait_recv()

    @pl.when(section != 0)
    def _():
        for h in range(PARTS):
            out_ref[:, h * part : (h + 1) * part] = arrive[h]

    @pl.when(section == 0)
    def _():
        squares = jnp.zeros((tokens, BLOCK), F32)
        for b in range(width // BLOCK):
            place = (b % per_part) * BLOCK
            values = arrive[b // per_part, :, place : place + BLOCK].astype(F32)
            squares = squares + values * values
        inverse = lax.rsqrt(jnp.sum(squares, axis=1, keepdims=True) / width + EPS)
        for b in range(width // BLOCK):
            place, cols = (b % per_part) * BLOCK, slice(b * BLOCK, (b + 1) * BLOCK)
            values = arrive[b // per_part, :, place : place + BLOCK].astype(F32)
            out_ref[:, cols] = (values * inverse * final_ref[:, cols]).astype(BF16)

    for h in range(PARTS):
        for step in range(FAR):
            for direction in range(2):
                gather(direction, step, h).wait_send()
                scatter(direction, step, h).wait_send()
        for c in range(FAR):
            dispatched(c, h).wait_send()
            given_back(c, h).wait_send()
        onward(h).wait_send()
    for step in range(FAR):
        for direction in range(2):
            gather_meta(direction, step).wait_send()


def local(pending, gain, final_gain, assigned, mixing, raising, lowering):
    x = pending[0]
    tokens, width = x.shape
    hidden = lowering.shape[2]
    part = width // PARTS
    vmem = pl.BlockSpec(memory_space=pltpu.VMEM)
    hbm = pl.BlockSpec(memory_space=pl.ANY)
    sems = pltpu.SemaphoreType.DMA
    arrived = pl.pallas_call(
        body,
        out_shape=jax.ShapeDtypeStruct((tokens, width), BF16),
        in_specs=[vmem, vmem, vmem, vmem, vmem, hbm, hbm],
        out_specs=vmem,
        scratch_shapes=[
            pltpu.VMEM((PARTS, NZ, tokens, part), BF16),
            pltpu.VMEM((NZ, tokens, LANES), BF16),
            pltpu.VMEM((PARTS, FAR, ROWS, part), BF16),
            pltpu.VMEM((PARTS, FAR, ROWS, part), BF16),
            pltpu.VMEM((PARTS, FAR, ROWS, part), BF16),
            pltpu.VMEM((PARTS, FAR, ROWS, part), BF16),
            pltpu.VMEM((FAR, 2 * tokens, ROWS), BF16),
            pltpu.VMEM((ROWS, 2 * tokens), BF16),
            pltpu.VMEM((4, LANES, ROWS), BF16),
            pltpu.VMEM((2, ROWS, LANES), BF16),
            pltpu.VMEM((width, 2 * hidden), BF16),
            pltpu.VMEM((hidden, width), BF16),
            pltpu.VMEM((ROWS, hidden), BF16),
            pltpu.VMEM((PARTS, tokens, part), F32),
            pltpu.VMEM((PARTS, NZ, tokens, part), BF16),
            pltpu.VMEM((PARTS, 2, FAR, tokens, part), BF16),
            pltpu.VMEM((PARTS, tokens, part), BF16),
            pltpu.VMEM((PARTS, tokens, part), BF16),
            sems((2, FAR, PARTS)),
            sems((2, FAR, PARTS)),
            sems((2, FAR)),
            sems((2, FAR)),
            sems((FAR, PARTS)),
            sems((FAR, PARTS)),
            sems((FAR, PARTS)),
            sems((FAR, PARTS)),
            sems((2, FAR, PARTS)),
            sems((2, FAR, PARTS)),
            sems((PARTS,)),
            sems((PARTS,)),
            sems((2,)),
        ],
        compiler_params=pltpu.CompilerParams(
            collective_id=0, has_side_effects=True, vmem_limit_bytes=62 << 20
        ),
        name="relay_step",
    )(x, gain, final_gain[None], assigned[0], mixing[0], raising[0, 0], lowering[0, 0])
    return arrived[None]


def solution(mesh):
    in_specs = (
        P("section", "expert", None),
        P("section", None),
        P(),
        P("section", "expert", None),
        P("section", "expert", None),
        P("section", "expert", None, None),
        P("section", "expert", None, None),
    )
    out_specs = P("section", "expert", None)
    return jax.shard_map(local, mesh=mesh, in_specs=in_specs, out_specs=out_specs, check_vma=False)
```

```python
import functools

import jax
import jax.numpy as jnp
from jax import lax
from jax.experimental import pallas as pl
from jax.experimental.pallas import tpu as pltpu
from jax.sharding import PartitionSpec as P

MESH = pl.DeviceIdType.MESH
F32, BF16 = jnp.float32, jnp.bfloat16
BLOCK = 128
EPS = 1e-06
NX, NY, NZ = 4, 2, 8
PLANE = NX * NY
FAR = NZ // 2
CAPACITY = 24
PAIR = 2 * CAPACITY
ROWS = PLANE * PAIR
PARTS = 4
TILE = 256
EARLY = 16
LANES = 128


def dot(a, b):
    return jnp.dot(a, b, preferred_element_type=F32)


def dot_nt(a, b):
    return lax.dot_general(a, b, (((1,), (1,)), ((), ())), preferred_element_type=F32)


def body(
    x_ref, gain_ref, final_ref, route_ref, mixing_ref, up_ref, down_ref, out_ref,
    line, meta, srow, rrow, orow, ret, erow, mix, pick, spread, spread_t, wup, wdown, hid,
    acc, rsout, rsin, layer, arrive,
    ag_send, ag_recv, am_send, am_recv, d_send, d_recv, r_send, r_recv,
    rs_send, rs_recv, sec_send, sec_recv, w_sem,
):
    tokens, width = x_ref.shape
    part = width // PARTS
    hidden = wdown.shape[0]
    top = route_ref.shape[0]
    per_part = part // BLOCK
    tiles = part // TILE
    experts = PLANE * NZ
    half = tokens // 2
    me = lax.axis_index("expert")
    section = lax.axis_index("section")
    sections = lax.axis_size("section")
    mx, my, mz = me // (NY * NZ), (me // NZ) % NY, me % NZ

    def in_plane(sign, offset):
        dx, dy = offset // NY, offset % NY
        return (((mx + sign * dx + NX) % NX) * NY + (my + dy) % NY) * NZ + mz

    column = me - mz
    around = (column + (mz + 1) % NZ, column + (mz + NZ - 1) % NZ)
    following = (section + 1) % sections
    previous = (section + sections - 1) % sections

    weights = [
        pltpu.make_async_copy(up_ref, wup, w_sem.at[0]),
        pltpu.make_async_copy(down_ref, wdown, w_sem.at[1]),
    ]
    for copy in weights:
        copy.start()

    barrier = pltpu.get_barrier_semaphore()

    def greet(offset, carry):
        pl.semaphore_signal(
            barrier, 1, device_id={"expert": in_plane(1, offset)}, device_id_type=MESH
        )
        return carry

    lax.fori_loop(1, PLANE, greet, 0)
    for peer in around:
        pl.semaphore_signal(barrier, 1, device_id={"expert": peer}, device_id_type=MESH)
    for peer in (following, previous):
        pl.semaphore_signal(barrier, 1, device_id={"section": peer}, device_id_type=MESH)

    def restore(h):
        for b in range(h * per_part, (h + 1) * per_part):
            cols = slice(b * BLOCK, (b + 1) * BLOCK)
            normed = x_ref[:, cols].astype(F32) * inverse * gain_ref[:, cols]
            scale = jnp.max(jnp.abs(normed), axis=1, keepdims=True) + EPS
            scale = scale.astype(BF16).astype(F32)
            quantized = (normed * (1.0 / scale)).astype(BF16).astype(F32)
            place = slice((b % per_part) * BLOCK, (b % per_part + 1) * BLOCK)
            line[h, 0, :, place] = (quantized * scale).astype(BF16)

    def route():
        lane = lax.broadcasted_iota(jnp.int32, (LANES, tokens), 0)
        named = jnp.zeros((LANES, tokens), F32)
        share = jnp.zeros((LANES, tokens), F32)
        for k in range(top):
            name = route_ref[k : k + 1, :]
            named = named + jnp.where(lane == name, 1.0, 0.0)
            share = share + jnp.where(lane - experts == name, mixing_ref[k : k + 1, :], 0.0)
        up_to = lax.broadcasted_iota(jnp.int32, (tokens, tokens), 0)
        up_to = up_to <= lax.broadcasted_iota(jnp.int32, (tokens, tokens), 1)
        place = dot(named.astype(BF16), jnp.where(up_to, 1.0, 0.0).astype(BF16))
        meta[0] = jnp.where(lane < experts, place * named, share).T.astype(BF16)

    def slots(shape, dim):
        q = lax.broadcasted_iota(jnp.int32, shape, dim)
        offset = jnp.zeros(shape, jnp.int32)
        for i in range(1, PLANE):
            offset = offset + jnp.where(q >= i * PAIR, 1, 0)
        q = q - offset * PAIR
        second = jnp.where(q >= CAPACITY, 1, 0)
        return offset, second, q - second * CAPACITY

    def owner(offset):
        dx, dy = offset >> 1, offset & 1
        return ((((mx + dx) & (NX - 1)) * NY) + ((my + dy) & (NY - 1))) * NZ + mz

    def spreads():
        offset, second, _ = slots((LANES, ROWS), 1)
        expert = owner(offset)
        lane_of = lax.broadcasted_iota(jnp.int32, (LANES, ROWS), 0)
        for i in range(2):
            for j in range(2):
                hit = (lane_of == expert + j * experts) & (second == i)
                spread[2 * j + i] = jnp.where(hit, 1.0, 0.0).astype(BF16)
        offset, second, _ = slots((ROWS, LANES), 0)
        expert = owner(offset)
        lane_of = lax.broadcasted_iota(jnp.int32, (ROWS, LANES), 1)
        for i in range(2):
            hit = (lane_of == expert) & (second == i)
            spread_t[i] = jnp.where(hit, 1.0, 0.0).astype(BF16)

    def early_pick():
        q = lax.broadcasted_iota(jnp.int32, (PLANE * EARLY, LANES), 0)
        lane_of = lax.broadcasted_iota(jnp.int32, (PLANE * EARLY, LANES), 1)
        named = jnp.where(lane_of == owner(q >> 4), 1.0, 0.0).astype(BF16)
        want = ((q & (EARLY - 1)) + 1).astype(F32)
        return jnp.where(dot_nt(named, meta[0]) == want, 1.0, 0.0).astype(BF16)

    def few(step, direction):
        if step < FAR - 1:
            return pl.ds(0, tokens)
        return pl.ds(direction * half, half)

    def gather(direction, step, h):
        source, target = ((NZ - step) % NZ, NZ - 1 - step) if direction == 0 else (step, step + 1)
        rows = few(step, direction)
        return pltpu.make_async_remote_copy(
            line.at[h, source, rows], line.at[h, target, rows],
            ag_send.at[direction, step, h], ag_recv.at[direction, step, h],
            device_id={"expert": around[direction]}, device_id_type=MESH,
        )

    def gather_meta(direction, step):
        source, target = ((NZ - step) % NZ, NZ - 1 - step) if direction == 0 else (step, step + 1)
        rows = few(step, direction)
        return pltpu.make_async_remote_copy(
            meta.at[source, rows], meta.at[target, rows],
            am_send.at[direction, step], am_recv.at[direction, step],
            device_id={"expert": around[direction]}, device_id_type=MESH,
        )

    def build(c, first, last):
        _, _, want = slots((ROWS, tokens), 0)
        want = (want + 1).astype(F32)
        for i, rel in enumerate((first, last)):
            found = dot_nt(spread_t[i], meta[rel])
            pick[:, i * tokens : (i + 1) * tokens] = jnp.where(found == want, 1.0, 0.0).astype(BF16)
        _, _, want = slots((tokens, ROWS), 1)
        want = (want + 1).astype(F32)
        for i, rel in enumerate((first, last)):
            found = dot(meta[rel], spread[i])
            weight = dot(meta[rel], spread[2 + i])
            mix[c, i * tokens : (i + 1) * tokens] = jnp.where(found == want, weight, 0.0).astype(BF16)

    def select(c, first, last, h):
        def tile(n, carry):
            cols = pl.ds(pl.multiple_of(n * TILE, TILE), TILE)
            both = jnp.concatenate([line[h, first, :, cols], line[h, last, :, cols]], axis=0)
            rows = dot(pick[...], both).astype(BF16)
            srow[h, c, :, cols] = rows
            rrow[h, c, pl.ds(0, PAIR), cols] = rows[:PAIR]
            return carry

        lax.fori_loop(0, tiles, tile, 0)

    def plane_copy(source, target, send, recv, sign, offset, c, h):
        rows = pl.ds(pl.multiple_of(offset * PAIR, 16), PAIR)
        return pltpu.make_async_remote_copy(
            source.at[h, c, rows], target.at[h, c, rows], send.at[c, h], recv.at[c, h],
            device_id={"expert": in_plane(sign, offset)}, device_id_type=MESH,
        )

    def plane_all(source, target, send, recv, c, h):
        rows = pl.ds(PAIR, ROWS - PAIR)
        return pltpu.make_async_remote_copy(
            source.at[h, c, rows], target.at[h, c, rows], send.at[c, h], recv.at[c, h],
            device_id={"expert": in_plane(1, 1)}, device_id_type=MESH,
        )

    def dispatch(c, h):
        def send(offset, carry):
            if c:
                plane_copy(srow, rrow, d_send, d_recv, 1, offset, c, h).start()
                return carry
            rows = pl.ds(pl.multiple_of(offset * PAIR + EARLY, 16), PAIR - EARLY)
            pltpu.make_async_remote_copy(
                srow.at[h, 0, rows], rrow.at[h, 0, rows], d_send.at[0, h], d_recv.at[0, h],
                device_id={"expert": in_plane(1, offset)}, device_id_type=MESH,
            ).start()
            return carry

        lax.fori_loop(1, PLANE, send, 0)

    def dispatch_early(h, chosen):
        erow[h] = dot(chosen, line[h, 0]).astype(BF16)

        def send(offset, carry):
            source = pl.ds(pl.multiple_of(offset * EARLY, 16), EARLY)
            target = pl.ds(pl.multiple_of(offset * PAIR, 16), EARLY)
            pltpu.make_async_remote_copy(
                erow.at[h, source], rrow.at[h, 0, target], d_send.at[0, h], d_recv.at[0, h],
                device_id={"expert": in_plane(1, offset)}, device_id_type=MESH,
            ).start()
            return carry

        lax.fori_loop(1, PLANE, send, 0)

    def give_back(c, h):
        def send(offset, carry):
            plane_copy(orow, ret, r_send, r_recv, -1, offset, c, h).start()
            return carry

        lax.fori_loop(1, PLANE, send, 0)

    dispatched = functools.partial(plane_all, srow, rrow, d_send, d_recv)
    given_back = functools.partial(plane_all, orow, ret, r_send, r_recv)

    def expert_rows(c):
        for h in range(PARTS):
            dispatched(c, h).wait_recv()

        def gate(n, carry):
            total = []
            for base in (0, hidden):
                cols = pl.ds(pl.multiple_of(base + n * TILE, TILE), TILE)
                total.append(
                    sum(dot(rrow[h, c], wup[pl.ds(h * part, part), cols]) for h in range(PARTS))
                )
            g, u = total
            cols = pl.ds(pl.multiple_of(n * TILE, TILE), TILE)
            hid[:, cols] = (g / (1.0 + jnp.exp(-g)) * u).astype(BF16)
            return carry

        lax.fori_loop(0, hidden // TILE, gate, 0)

        def lower(n, carry):
            wide = pl.ds(pl.multiple_of(n * TILE, TILE), TILE)
            cols = pl.ds(pl.multiple_of((n % tiles) * TILE, TILE), TILE)
            rows = dot(hid[...], wdown[:, wide]).astype(BF16)
            orow[n // tiles, c, :, cols] = rows
            ret[n // tiles, c, pl.ds(0, PAIR), cols] = rows[:PAIR]
            return carry

        lax.fori_loop(0, PARTS * tiles, lower, 0)

    def scatter(direction, step, h):
        source = FAR - step if direction == 0 else FAR + step
        rows = pl.ds(0, tokens) if step else pl.ds(direction * half, half)
        return pltpu.make_async_remote_copy(
            rsout.at[h, source, rows], rsin.at[h, direction, step, rows],
            rs_send.at[direction, step, h], rs_recv.at[direction, step, h],
            device_id={"expert": around[direction]}, device_id_type=MESH,
        )

    def combine(c, h):
        step = FAR - c if c else 0
        given_back(c, h).wait_recv()
        if step:
            for direction in range(2):
                scatter(direction, step - 1, h).wait_recv()

        def tile(n, carry):
            cols = pl.ds(pl.multiple_of(n * TILE, TILE), TILE)
            wide = pl.ds(pl.multiple_of(h * part + n * TILE, TILE), TILE)
            sums = dot(mix[c], ret[h, c, :, cols])
            near, away = sums[:tokens], sums[tokens:]
            if step == 0:
                acc[h, :, cols] = near + x_ref[:, wide].astype(F32)
                rsout[h, FAR, :, cols] = away.astype(BF16)
                return carry
            if step == 1:
                low, high = pl.ds(0, half), pl.ds(half, half)
                rsout[h, c, low, cols] = (near[:half] + rsin[h, 0, 0, low, cols].astype(F32)).astype(BF16)
                rsout[h, c, high, cols] = near[half:].astype(BF16)
                rsout[h, NZ - c, low, cols] = away[:half].astype(BF16)
                rsout[h, NZ - c, high, cols] = (away[half:] + rsin[h, 1, 0, high, cols].astype(F32)).astype(BF16)
                return carry
            rsout[h, c, :, cols] = (near + rsin[h, 0, step - 1, :, cols].astype(F32)).astype(BF16)
            rsout[h, NZ - c, :, cols] = (away + rsin[h, 1, step - 1, :, cols].astype(F32)).astype(BF16)
            return carry

        lax.fori_loop(0, tiles, tile, 0)
        for direction in range(2):
            scatter(direction, step, h).start()

    def onward(h):
        return pltpu.make_async_remote_copy(
            layer.at[h], arrive.at[h], sec_send.at[h], sec_recv.at[h],
            device_id={"section": following}, device_id_type=MESH,
        )

    squares = jnp.zeros((tokens, BLOCK), F32)
    for b in range(width // BLOCK):
        values = x_ref[:, b * BLOCK : (b + 1) * BLOCK].astype(F32)
        squares = squares + values * values
    inverse = lax.rsqrt(jnp.sum(squares, axis=1, keepdims=True) / width + EPS)
    restore(0)
    route()
    pl.semaphore_wait(barrier, PLANE - 1 + 4)
    for h in range(PARTS):
        if h:
            restore(h)
        for direction in range(2):
            gather(direction, 0, h).start()
            if h == 0:
                gather_meta(direction, 0).start()
        if h == 0:
            chosen = early_pick()
        dispatch_early(h, chosen)
    spreads()
    for step in range(1, FAR + 1):
        c = step % FAR
        first, last = (step, NZ - step) if c else (0, FAR)
        for direction in range(2):
            gather_meta(direction, step - 1).wait_recv()
            if c:
                gather_meta(direction, step).start()
        build(c, first, last)
        for h in range(PARTS):
            for direction in range(2):
                gather(direction, step - 1, h).wait_recv()
                if c:
                    gather(direction, step, h).start()
            select(c, first, last, h)
            dispatch(c, h)

    for copy in weights:
        copy.wait()
    for c in range(1, FAR):
        expert_rows(c)
    for h in range(PARTS):
        give_back(FAR - 1, h)
    expert_rows(0)
    for h in range(PARTS):
        give_back(0, h)
    for c in range(FAR - 2, 0, -1):
        for h in range(PARTS):
            give_back(c, h)
    for c in (0, *range(FAR - 1, 0, -1)):
        for h in range(PARTS):
            combine(c, h)
    for h in range(PARTS):
        for direction in range(2):
            scatter(direction, FAR - 1, h).wait_recv()
        total = acc[h] + rsin[h, 0, FAR - 1].astype(F32) + rsin[h, 1, FAR - 1].astype(F32)
        layer[h] = total.astype(BF16)
        onward(h).start()
    for h in range(PARTS):
        onward(h).wait_recv()

    @pl.when(section != 0)
    def _():
        for h in range(PARTS):
            out_ref[:, h * part : (h + 1) * part] = arrive[h]

    @pl.when(section == 0)
    def _():
        squares = jnp.zeros((tokens, BLOCK), F32)
        for b in range(width // BLOCK):
            place = (b % per_part) * BLOCK
            values = arrive[b // per_part, :, place : place + BLOCK].astype(F32)
            squares = squares + values * values
        inverse = lax.rsqrt(jnp.sum(squares, axis=1, keepdims=True) / width + EPS)
        for b in range(width // BLOCK):
            place, cols = (b % per_part) * BLOCK, slice(b * BLOCK, (b + 1) * BLOCK)
            values = arrive[b // per_part, :, place : place + BLOCK].astype(F32)
            out_ref[:, cols] = (values * inverse * final_ref[:, cols]).astype(BF16)

    for h in range(PARTS):
        for step in range(FAR):
            for direction in range(2):
                gather(direction, step, h).wait_send()
                scatter(direction, step, h).wait_send()
        for c in range(FAR):
            dispatched(c, h).wait_send()
            given_back(c, h).wait_send()
        onward(h).wait_send()
    for step in range(FAR):
        for direction in range(2):
            gather_meta(direction, step).wait_send()


def local(pending, gain, final_gain, assigned, mixing, raising, lowering):
    x = pending[0]
    tokens, width = x.shape
    hidden = lowering.shape[2]
    part = width // PARTS
    vmem = pl.BlockSpec(memory_space=pltpu.VMEM)
    hbm = pl.BlockSpec(memory_space=pl.ANY)
    sems = pltpu.SemaphoreType.DMA
    arrived = pl.pallas_call(
        body,
        out_shape=jax.ShapeDtypeStruct((tokens, width), BF16),
        in_specs=[vmem, vmem, vmem, vmem, vmem, hbm, hbm],
        out_specs=vmem,
        scratch_shapes=[
            pltpu.VMEM((PARTS, NZ, tokens, part), BF16),
            pltpu.VMEM((NZ, tokens, LANES), BF16),
            pltpu.VMEM((PARTS, FAR, ROWS, part), BF16),
            pltpu.VMEM((PARTS, FAR, ROWS, part), BF16),
            pltpu.VMEM((PARTS, FAR, ROWS, part), BF16),
            pltpu.VMEM((PARTS, FAR, ROWS, part), BF16),
            pltpu.VMEM((PARTS, PLANE * EARLY, part), BF16),
            pltpu.VMEM((FAR, 2 * tokens, ROWS), BF16),
            pltpu.VMEM((ROWS, 2 * tokens), BF16),
            pltpu.VMEM((4, LANES, ROWS), BF16),
            pltpu.VMEM((2, ROWS, LANES), BF16),
            pltpu.VMEM((width, 2 * hidden), BF16),
            pltpu.VMEM((hidden, width), BF16),
            pltpu.VMEM((ROWS, hidden), BF16),
            pltpu.VMEM((PARTS, tokens, part), F32),
            pltpu.VMEM((PARTS, NZ, tokens, part), BF16),
            pltpu.VMEM((PARTS, 2, FAR, tokens, part), BF16),
            pltpu.VMEM((PARTS, tokens, part), BF16),
            pltpu.VMEM((PARTS, tokens, part), BF16),
            sems((2, FAR, PARTS)),
            sems((2, FAR, PARTS)),
            sems((2, FAR)),
            sems((2, FAR)),
            sems((FAR, PARTS)),
            sems((FAR, PARTS)),
            sems((FAR, PARTS)),
            sems((FAR, PARTS)),
            sems((2, FAR, PARTS)),
            sems((2, FAR, PARTS)),
            sems((PARTS,)),
            sems((PARTS,)),
            sems((2,)),
        ],
        compiler_params=pltpu.CompilerParams(
            collective_id=0, has_side_effects=True, vmem_limit_bytes=62 << 20
        ),
        name="relay_step",
    )(x, gain, final_gain[None], assigned[0].T, mixing[0].T, raising[0, 0], lowering[0, 0])
    return arrived[None]


def solution(mesh):
    in_specs = (
        P("section", "expert", None),
        P("section", None),
        P(),
        P("section", "expert", None),
        P("section", "expert", None),
        P("section", "expert", None, None),
        P("section", "expert", None, None),
    )
    out_specs = P("section", "expert", None)
    return jax.shard_map(local, mesh=mesh, in_specs=in_specs, out_specs=out_specs, check_vma=False)
```

```python
import functools

import jax
import jax.numpy as jnp
from jax import lax
from jax.experimental import pallas as pl
from jax.experimental.pallas import tpu as pltpu
from jax.sharding import PartitionSpec as P

MESH = pl.DeviceIdType.MESH
F32, BF16 = jnp.float32, jnp.bfloat16
BLOCK = 128
EPS = 1e-06
NX, NY, NZ = 4, 2, 8
PLANE = NX * NY
FAR = NZ // 2
CAPACITY = 24
PAIR = 2 * CAPACITY
ROWS = PLANE * PAIR
PARTS = 4
TILE = 256
EARLY = 16
LANES = 128


def dot(a, b):
    return jnp.dot(a, b, preferred_element_type=F32)


def dot_nt(a, b):
    return lax.dot_general(a, b, (((1,), (1,)), ((), ())), preferred_element_type=F32)


def body(
    x_ref, gain_ref, final_ref, route_ref, mixing_ref, up_ref, down_ref, out_ref,
    line, meta, srow, rrow, orow, ret, erow, lret, mix, mix_late, pick, spread, spread_t, wup, wdown, hid,
    acc, rsout, rsin, layer, arrive,
    ag_send, ag_recv, am_send, am_recv, d_send, d_recv, r_send, r_recv,
    rs_send, rs_recv, sec_send, sec_recv, l_send, l_recv, w_sem,
):
    tokens, width = x_ref.shape
    part = width // PARTS
    hidden = wdown.shape[0]
    top = route_ref.shape[0]
    per_part = part // BLOCK
    tiles = part // TILE
    experts = PLANE * NZ
    half = tokens // 2
    me = lax.axis_index("expert")
    section = lax.axis_index("section")
    sections = lax.axis_size("section")
    mx, my, mz = me // (NY * NZ), (me // NZ) % NY, me % NZ

    def in_plane(sign, offset):
        dx, dy = offset // NY, offset % NY
        return (((mx + sign * dx + NX) % NX) * NY + (my + dy) % NY) * NZ + mz

    column = me - mz
    around = (column + (mz + 1) % NZ, column + (mz + NZ - 1) % NZ)
    following = (section + 1) % sections
    previous = (section + sections - 1) % sections

    weights = [
        pltpu.make_async_copy(up_ref, wup, w_sem.at[0]),
        pltpu.make_async_copy(down_ref, wdown, w_sem.at[1]),
    ]
    for copy in weights:
        copy.start()

    barrier = pltpu.get_barrier_semaphore()

    def greet(offset, carry):
        pl.semaphore_signal(
            barrier, 1, device_id={"expert": in_plane(1, offset)}, device_id_type=MESH
        )
        return carry

    lax.fori_loop(1, PLANE, greet, 0)
    for peer in around:
        pl.semaphore_signal(barrier, 1, device_id={"expert": peer}, device_id_type=MESH)
    for peer in (following, previous):
        pl.semaphore_signal(barrier, 1, device_id={"section": peer}, device_id_type=MESH)

    def restore(h):
        for b in range(h * per_part, (h + 1) * per_part):
            cols = slice(b * BLOCK, (b + 1) * BLOCK)
            normed = x_ref[:, cols].astype(F32) * inverse * gain_ref[:, cols]
            scale = jnp.max(jnp.abs(normed), axis=1, keepdims=True) + EPS
            scale = scale.astype(BF16).astype(F32)
            quantized = (normed * (1.0 / scale)).astype(BF16).astype(F32)
            place = slice((b % per_part) * BLOCK, (b % per_part + 1) * BLOCK)
            line[h, 0, :, place] = (quantized * scale).astype(BF16)

    def route():
        lane = lax.broadcasted_iota(jnp.int32, (LANES, tokens), 0)
        named = jnp.zeros((LANES, tokens), F32)
        share = jnp.zeros((LANES, tokens), F32)
        for k in range(top):
            name = route_ref[k : k + 1, :]
            named = named + jnp.where(lane == name, 1.0, 0.0)
            share = share + jnp.where(lane - experts == name, mixing_ref[k : k + 1, :], 0.0)
        up_to = lax.broadcasted_iota(jnp.int32, (tokens, tokens), 0)
        up_to = up_to <= lax.broadcasted_iota(jnp.int32, (tokens, tokens), 1)
        place = dot(named.astype(BF16), jnp.where(up_to, 1.0, 0.0).astype(BF16))
        meta[0] = jnp.where(lane < experts, place * named, share).T.astype(BF16)

    def slots(shape, dim):
        q = lax.broadcasted_iota(jnp.int32, shape, dim)
        offset = jnp.zeros(shape, jnp.int32)
        for i in range(1, PLANE):
            offset = offset + jnp.where(q >= i * PAIR, 1, 0)
        q = q - offset * PAIR
        second = jnp.where(q >= CAPACITY, 1, 0)
        return offset, second, q - second * CAPACITY

    def owner(offset):
        dx, dy = offset >> 1, offset & 1
        return ((((mx + dx) & (NX - 1)) * NY) + ((my + dy) & (NY - 1))) * NZ + mz

    def spreads():
        offset, second, _ = slots((LANES, ROWS), 1)
        expert = owner(offset)
        lane_of = lax.broadcasted_iota(jnp.int32, (LANES, ROWS), 0)
        for i in range(2):
            for j in range(2):
                hit = (lane_of == expert + j * experts) & (second == i)
                spread[2 * j + i] = jnp.where(hit, 1.0, 0.0).astype(BF16)
        offset, second, _ = slots((ROWS, LANES), 0)
        expert = owner(offset)
        lane_of = lax.broadcasted_iota(jnp.int32, (ROWS, LANES), 1)
        for i in range(2):
            hit = (lane_of == expert) & (second == i)
            spread_t[i] = jnp.where(hit, 1.0, 0.0).astype(BF16)

    def early_pick():
        q = lax.broadcasted_iota(jnp.int32, (PLANE * EARLY, LANES), 0)
        lane_of = lax.broadcasted_iota(jnp.int32, (PLANE * EARLY, LANES), 1)
        named = jnp.where(lane_of == owner(q >> 4), 1.0, 0.0).astype(BF16)
        want = ((q & (EARLY - 1)) + 1).astype(F32)
        return jnp.where(dot_nt(named, meta[0]) == want, 1.0, 0.0).astype(BF16)

    def late_mix():
        shape = (LANES, PLANE * EARLY)
        q, lane_of = lax.broadcasted_iota(jnp.int32, shape, 1), lax.broadcasted_iota(jnp.int32, shape, 0)
        expert = owner(q >> 4)
        named = jnp.where(lane_of == expert, 1.0, 0.0).astype(BF16)
        share = jnp.where(lane_of == expert + experts, 1.0, 0.0).astype(BF16)
        q = lax.broadcasted_iota(jnp.int32, (tokens, PLANE * EARLY), 1)
        want = ((q & (EARLY - 1)) + 1).astype(F32)
        weight = dot(meta[0], share)
        mix_late[...] = jnp.where(dot(meta[0], named) == want, weight, 0.0).astype(BF16)
        for h in range(PARTS):
            lret[h, pl.ds(0, EARLY)] = jnp.zeros((EARLY, part), BF16)
            for offset in range(1, PLANE):
                ret[h, 0, pl.ds(offset * PAIR, EARLY)] = jnp.zeros((EARLY, part), BF16)

    def few(step, direction):
        if step < FAR - 1:
            return pl.ds(0, tokens)
        return pl.ds(direction * half, half)

    def gather(direction, step, h):
        source, target = ((NZ - step) % NZ, NZ - 1 - step) if direction == 0 else (step, step + 1)
        rows = few(step, direction)
        return pltpu.make_async_remote_copy(
            line.at[h, source, rows], line.at[h, target, rows],
            ag_send.at[direction, step, h], ag_recv.at[direction, step, h],
            device_id={"expert": around[direction]}, device_id_type=MESH,
        )

    def gather_meta(direction, step):
        source, target = ((NZ - step) % NZ, NZ - 1 - step) if direction == 0 else (step, step + 1)
        rows = few(step, direction)
        return pltpu.make_async_remote_copy(
            meta.at[source, rows], meta.at[target, rows],
            am_send.at[direction, step], am_recv.at[direction, step],
            device_id={"expert": around[direction]}, device_id_type=MESH,
        )

    def build(c, first, last):
        _, _, want = slots((ROWS, tokens), 0)
        want = (want + 1).astype(F32)
        for i, rel in enumerate((first, last)):
            found = dot_nt(spread_t[i], meta[rel])
            pick[:, i * tokens : (i + 1) * tokens] = jnp.where(found == want, 1.0, 0.0).astype(BF16)
        _, _, want = slots((tokens, ROWS), 1)
        want = (want + 1).astype(F32)
        for i, rel in enumerate((first, last)):
            found = dot(meta[rel], spread[i])
            weight = dot(meta[rel], spread[2 + i])
            mix[c, i * tokens : (i + 1) * tokens] = jnp.where(found == want, weight, 0.0).astype(BF16)

    def select(c, first, last, h):
        def tile(n, carry):
            cols = pl.ds(pl.multiple_of(n * TILE, TILE), TILE)
            both = jnp.concatenate([line[h, first, :, cols], line[h, last, :, cols]], axis=0)
            rows = dot(pick[...], both).astype(BF16)
            srow[h, c, :, cols] = rows
            rrow[h, c, pl.ds(0, PAIR), cols] = rows[:PAIR]
            return carry

        lax.fori_loop(0, tiles, tile, 0)

    def plane_copy(source, target, send, recv, sign, offset, c, h):
        rows = pl.ds(pl.multiple_of(offset * PAIR, 16), PAIR)
        return pltpu.make_async_remote_copy(
            source.at[h, c, rows], target.at[h, c, rows], send.at[c, h], recv.at[c, h],
            device_id={"expert": in_plane(sign, offset)}, device_id_type=MESH,
        )

    def plane_all(source, target, send, recv, c, h):
        rows = pl.ds(PAIR, ROWS - PAIR)
        return pltpu.make_async_remote_copy(
            source.at[h, c, rows], target.at[h, c, rows], send.at[c, h], recv.at[c, h],
            device_id={"expert": in_plane(1, 1)}, device_id_type=MESH,
        )

    def dispatch(c, h):
        def send(offset, carry):
            if c:
                plane_copy(srow, rrow, d_send, d_recv, 1, offset, c, h).start()
                return carry
            rows = pl.ds(pl.multiple_of(offset * PAIR + EARLY, 16), PAIR - EARLY)
            pltpu.make_async_remote_copy(
                srow.at[h, 0, rows], rrow.at[h, 0, rows], d_send.at[0, h], d_recv.at[0, h],
                device_id={"expert": in_plane(1, offset)}, device_id_type=MESH,
            ).start()
            return carry

        lax.fori_loop(1, PLANE, send, 0)

    def dispatch_early(h, chosen):
        erow[h] = dot(chosen, line[h, 0]).astype(BF16)

        def send(offset, carry):
            source = pl.ds(pl.multiple_of(offset * EARLY, 16), EARLY)
            target = pl.ds(pl.multiple_of(offset * PAIR, 16), EARLY)
            pltpu.make_async_remote_copy(
                erow.at[h, source], rrow.at[h, 0, target], d_send.at[0, h], d_recv.at[0, h],
                device_id={"expert": in_plane(1, offset)}, device_id_type=MESH,
            ).start()
            return carry

        lax.fori_loop(1, PLANE, send, 0)

    def give_back(c, h):
        def send(offset, carry):
            if c:
                plane_copy(orow, ret, r_send, r_recv, -1, offset, c, h).start()
                return carry
            rows = pl.ds(pl.multiple_of(offset * PAIR + EARLY, 16), PAIR - EARLY)
            pltpu.make_async_remote_copy(
                orow.at[h, 0, rows], ret.at[h, 0, rows], r_send.at[0, h], r_recv.at[0, h],
                device_id={"expert": in_plane(-1, offset)}, device_id_type=MESH,
            ).start()
            return carry

        lax.fori_loop(1, PLANE, send, 0)

    def late_copy(offset, h):
        source = pl.ds(pl.multiple_of(offset * PAIR, 16), EARLY)
        target = pl.ds(pl.multiple_of(offset * EARLY, 16), EARLY)
        return pltpu.make_async_remote_copy(
            orow.at[h, 0, source], lret.at[h, target], l_send.at[h], l_recv.at[h],
            device_id={"expert": in_plane(-1, offset)}, device_id_type=MESH,
        )

    def give_back_late(h):
        def send(offset, carry):
            late_copy(offset, h).start()
            return carry

        lax.fori_loop(1, PLANE, send, 0)

    def late(h):
        rows, few = pl.ds(EARLY, (PLANE - 1) * EARLY), pl.ds(PAIR, (PLANE - 1) * EARLY)
        return pltpu.make_async_remote_copy(
            orow.at[h, 0, few], lret.at[h, rows], l_send.at[h], l_recv.at[h],
            device_id={"expert": in_plane(-1, 1)}, device_id_type=MESH,
        )

    def returned(c, h):
        if c:
            return plane_all(orow, ret, r_send, r_recv, c, h)
        rows = pl.ds(PAIR, (PLANE - 1) * (PAIR - EARLY))
        return pltpu.make_async_remote_copy(
            orow.at[h, 0, rows], ret.at[h, 0, rows], r_send.at[0, h], r_recv.at[0, h],
            device_id={"expert": in_plane(-1, 1)}, device_id_type=MESH,
        )

    dispatched = functools.partial(plane_all, srow, rrow, d_send, d_recv)

    def expert_rows(c):
        for h in range(PARTS):
            dispatched(c, h).wait_recv()

        def gate(n, carry):
            total = []
            for base in (0, hidden):
                cols = pl.ds(pl.multiple_of(base + n * TILE, TILE), TILE)
                total.append(
                    sum(dot(rrow[h, c], wup[pl.ds(h * part, part), cols]) for h in range(PARTS))
                )
            g, u = total
            cols = pl.ds(pl.multiple_of(n * TILE, TILE), TILE)
            hid[:, cols] = (g / (1.0 + jnp.exp(-g)) * u).astype(BF16)
            return carry

        lax.fori_loop(0, hidden // TILE, gate, 0)

        def lower(n, carry):
            wide = pl.ds(pl.multiple_of(n * TILE, TILE), TILE)
            cols = pl.ds(pl.multiple_of((n % tiles) * TILE, TILE), TILE)
            rows = dot(hid[...], wdown[:, wide]).astype(BF16)
            orow[n // tiles, c, :, cols] = rows
            ret[n // tiles, c, pl.ds(0, PAIR), cols] = rows[:PAIR]
            return carry

        lax.fori_loop(0, PARTS * tiles, lower, 0)

    def scatter(direction, step, h):
        source = FAR - step if direction == 0 else FAR + step
        rows = pl.ds(0, tokens) if step else pl.ds(direction * half, half)
        return pltpu.make_async_remote_copy(
            rsout.at[h, source, rows], rsin.at[h, direction, step, rows],
            rs_send.at[direction, step, h], rs_recv.at[direction, step, h],
            device_id={"expert": around[direction]}, device_id_type=MESH,
        )

    def combine(c, h):
        step = FAR - c if c else 0
        returned(c, h).wait_recv()
        if step:
            for direction in range(2):
                scatter(direction, step - 1, h).wait_recv()

        def tile(n, carry):
            cols = pl.ds(pl.multiple_of(n * TILE, TILE), TILE)
            wide = pl.ds(pl.multiple_of(h * part + n * TILE, TILE), TILE)
            sums = dot(mix[c], ret[h, c, :, cols])
            near, away = sums[:tokens], sums[tokens:]
            if step == 0:
                acc[h, :, cols] = near + x_ref[:, wide].astype(F32)
                rsout[h, FAR, :, cols] = away.astype(BF16)
                return carry
            if step == 1:
                low, high = pl.ds(0, half), pl.ds(half, half)
                rsout[h, c, low, cols] = (near[:half] + rsin[h, 0, 0, low, cols].astype(F32)).astype(BF16)
                rsout[h, c, high, cols] = near[half:].astype(BF16)
                rsout[h, NZ - c, low, cols] = away[:half].astype(BF16)
                rsout[h, NZ - c, high, cols] = (away[half:] + rsin[h, 1, 0, high, cols].astype(F32)).astype(BF16)
                return carry
            rsout[h, c, :, cols] = (near + rsin[h, 0, step - 1, :, cols].astype(F32)).astype(BF16)
            rsout[h, NZ - c, :, cols] = (away + rsin[h, 1, step - 1, :, cols].astype(F32)).astype(BF16)
            return carry

        lax.fori_loop(0, tiles, tile, 0)
        for direction in range(2):
            scatter(direction, step, h).start()

    def onward(h):
        return pltpu.make_async_remote_copy(
            layer.at[h], arrive.at[h], sec_send.at[h], sec_recv.at[h],
            device_id={"section": following}, device_id_type=MESH,
        )

    squares = jnp.zeros((tokens, BLOCK), F32)
    for b in range(width // BLOCK):
        values = x_ref[:, b * BLOCK : (b + 1) * BLOCK].astype(F32)
        squares = squares + values * values
    inverse = lax.rsqrt(jnp.sum(squares, axis=1, keepdims=True) / width + EPS)
    restore(0)
    route()
    pl.semaphore_wait(barrier, PLANE - 1 + 4)
    for h in range(PARTS):
        if h:
            restore(h)
        for direction in range(2):
            gather(direction, 0, h).start()
            if h == 0:
                gather_meta(direction, 0).start()
        if h == 0:
            chosen = early_pick()
        dispatch_early(h, chosen)
    spreads()
    late_mix()
    for step in range(1, FAR + 1):
        c = step % FAR
        first, last = (step, NZ - step) if c else (0, FAR)
        for direction in range(2):
            gather_meta(direction, step - 1).wait_recv()
            if c:
                gather_meta(direction, step).start()
        build(c, first, last)
        for h in range(PARTS):
            for direction in range(2):
                gather(direction, step - 1, h).wait_recv()
                if c:
                    gather(direction, step, h).start()
            select(c, first, last, h)
            dispatch(c, h)

    for copy in weights:
        copy.wait()
    for c in range(1, FAR):
        expert_rows(c)
    for h in range(PARTS):
        give_back(FAR - 1, h)
    expert_rows(0)
    for h in range(PARTS):
        give_back(0, h)
    for c in range(FAR - 2, 0, -1):
        for h in range(PARTS):
            give_back(c, h)
    for h in range(PARTS):
        give_back_late(h)
    for c in (0, *range(FAR - 1, 0, -1)):
        for h in range(PARTS):
            combine(c, h)
    for h in range(PARTS):
        for direction in range(2):
            scatter(direction, FAR - 1, h).wait_recv()
        total = acc[h] + rsin[h, 0, FAR - 1].astype(F32) + rsin[h, 1, FAR - 1].astype(F32)
        late(h).wait_recv()
        total = total + dot(mix_late[...], lret[h])
        layer[h] = total.astype(BF16)
        onward(h).start()
    for h in range(PARTS):
        onward(h).wait_recv()

    @pl.when(section != 0)
    def _():
        for h in range(PARTS):
            out_ref[:, h * part : (h + 1) * part] = arrive[h]

    @pl.when(section == 0)
    def _():
        squares = jnp.zeros((tokens, BLOCK), F32)
        for b in range(width // BLOCK):
            place = (b % per_part) * BLOCK
            values = arrive[b // per_part, :, place : place + BLOCK].astype(F32)
            squares = squares + values * values
        inverse = lax.rsqrt(jnp.sum(squares, axis=1, keepdims=True) / width + EPS)
        for b in range(width // BLOCK):
            place, cols = (b % per_part) * BLOCK, slice(b * BLOCK, (b + 1) * BLOCK)
            values = arrive[b // per_part, :, place : place + BLOCK].astype(F32)
            out_ref[:, cols] = (values * inverse * final_ref[:, cols]).astype(BF16)

    for h in range(PARTS):
        for step in range(FAR):
            for direction in range(2):
                gather(direction, step, h).wait_send()
                scatter(direction, step, h).wait_send()
        for c in range(FAR):
            dispatched(c, h).wait_send()
            returned(c, h).wait_send()
        onward(h).wait_send()
        late(h).wait_send()
    for step in range(FAR):
        for direction in range(2):
            gather_meta(direction, step).wait_send()


def local(pending, gain, final_gain, assigned, mixing, raising, lowering):
    x = pending[0]
    tokens, width = x.shape
    hidden = lowering.shape[2]
    part = width // PARTS
    vmem = pl.BlockSpec(memory_space=pltpu.VMEM)
    hbm = pl.BlockSpec(memory_space=pl.ANY)
    sems = pltpu.SemaphoreType.DMA
    arrived = pl.pallas_call(
        body,
        out_shape=jax.ShapeDtypeStruct((tokens, width), BF16),
        in_specs=[vmem, vmem, vmem, vmem, vmem, hbm, hbm],
        out_specs=vmem,
        scratch_shapes=[
            pltpu.VMEM((PARTS, NZ, tokens, part), BF16),
            pltpu.VMEM((NZ, tokens, LANES), BF16),
            pltpu.VMEM((PARTS, FAR, ROWS, part), BF16),
            pltpu.VMEM((PARTS, FAR, ROWS, part), BF16),
            pltpu.VMEM((PARTS, FAR, ROWS, part), BF16),
            pltpu.VMEM((PARTS, FAR, ROWS, part), BF16),
            pltpu.VMEM((PARTS, PLANE * EARLY, part), BF16),
            pltpu.VMEM((PARTS, PLANE * EARLY, part), BF16),
            pltpu.VMEM((FAR, 2 * tokens, ROWS), BF16),
            pltpu.VMEM((tokens, PLANE * EARLY), BF16),
            pltpu.VMEM((ROWS, 2 * tokens), BF16),
            pltpu.VMEM((4, LANES, ROWS), BF16),
            pltpu.VMEM((2, ROWS, LANES), BF16),
            pltpu.VMEM((width, 2 * hidden), BF16),
            pltpu.VMEM((hidden, width), BF16),
            pltpu.VMEM((ROWS, hidden), BF16),
            pltpu.VMEM((PARTS, tokens, part), F32),
            pltpu.VMEM((PARTS, NZ, tokens, part), BF16),
            pltpu.VMEM((PARTS, 2, FAR, tokens, part), BF16),
            pltpu.VMEM((PARTS, tokens, part), BF16),
            pltpu.VMEM((PARTS, tokens, part), BF16),
            sems((2, FAR, PARTS)),
            sems((2, FAR, PARTS)),
            sems((2, FAR)),
            sems((2, FAR)),
            sems((FAR, PARTS)),
            sems((FAR, PARTS)),
            sems((FAR, PARTS)),
            sems((FAR, PARTS)),
            sems((2, FAR, PARTS)),
            sems((2, FAR, PARTS)),
            sems((PARTS,)),
            sems((PARTS,)),
            sems((PARTS,)),
            sems((PARTS,)),
            sems((2,)),
        ],
        compiler_params=pltpu.CompilerParams(
            collective_id=0, has_side_effects=True, vmem_limit_bytes=62 << 20
        ),
        name="relay_step",
    )(x, gain, final_gain[None], assigned[0].T, mixing[0].T, raising[0, 0], lowering[0, 0])
    return arrived[None]


def solution(mesh):
    in_specs = (
        P("section", "expert", None),
        P("section", None),
        P(),
        P("section", "expert", None),
        P("section", "expert", None),
        P("section", "expert", None, None),
        P("section", "expert", None, None),
    )
    out_specs = P("section", "expert", None)
    return jax.shard_map(local, mesh=mesh, in_specs=in_specs, out_specs=out_specs, check_vma=False)
```

```python
import functools

import jax
import jax.numpy as jnp
from jax import lax
from jax.experimental import pallas as pl
from jax.experimental.pallas import tpu as pltpu
from jax.sharding import PartitionSpec as P

MESH = pl.DeviceIdType.MESH
F32, BF16 = jnp.float32, jnp.bfloat16
BLOCK = 128
EPS = 1e-06
NX, NY, NZ = 4, 2, 8
PLANE = NX * NY
FAR = NZ // 2
CAPACITY = 24
PAIR = 2 * CAPACITY
ROWS = PLANE * PAIR
PARTS = 4
TILE = 256
EARLY = 16
LANES = 128


def dot(a, b):
    return jnp.dot(a, b, preferred_element_type=F32)


def dot_nt(a, b):
    return lax.dot_general(a, b, (((1,), (1,)), ((), ())), preferred_element_type=F32)


def body(
    x_hbm, gain_ref, final_ref, route_ref, mixing_ref, up_ref, down_ref, out_ref,
    x_ref, line, meta, srow, rrow, orow, ret, erow, lret, mix, mix_late, pick, spread, spread_t, wup, wdown, hid,
    acc, rsout, rsin, layer, arrive, normed,
    ag_send, ag_recv, am_send, am_recv, d_send, d_recv, r_send, r_recv,
    rs_send, rs_recv, sec_send, sec_recv, l_send, l_recv, o_sem, w_sem,
):
    tokens, width = x_ref.shape
    part = width // PARTS
    hidden = wdown.shape[0]
    top = route_ref.shape[0]
    per_part = part // BLOCK
    tiles = part // TILE
    experts = PLANE * NZ
    half = tokens // 2
    me = lax.axis_index("expert")
    section = lax.axis_index("section")
    sections = lax.axis_size("section")
    mx, my, mz = me // (NY * NZ), (me // NZ) % NY, me % NZ

    def in_plane(sign, offset):
        dx, dy = offset // NY, offset % NY
        return (((mx + sign * dx + NX) % NX) * NY + (my + dy) % NY) * NZ + mz

    column = me - mz
    around = (column + (mz + 1) % NZ, column + (mz + NZ - 1) % NZ)
    following = (section + 1) % sections
    previous = (section + sections - 1) % sections

    load = pltpu.make_async_copy(x_hbm, x_ref, w_sem.at[2])
    load.start()
    weights = [
        pltpu.make_async_copy(up_ref, wup, w_sem.at[0]),
        pltpu.make_async_copy(down_ref, wdown, w_sem.at[1]),
    ]

    barrier = pltpu.get_barrier_semaphore()

    def greet(offset, carry):
        pl.semaphore_signal(
            barrier, 1, device_id={"expert": in_plane(1, offset)}, device_id_type=MESH
        )
        return carry

    lax.fori_loop(1, PLANE, greet, 0)
    for peer in around:
        pl.semaphore_signal(barrier, 1, device_id={"expert": peer}, device_id_type=MESH)
    for peer in (following, previous):
        pl.semaphore_signal(barrier, 1, device_id={"section": peer}, device_id_type=MESH)

    def restore(h):
        for b in range(h * per_part, (h + 1) * per_part):
            cols = slice(b * BLOCK, (b + 1) * BLOCK)
            normed = x_ref[:, cols].astype(F32) * inverse * gain_ref[:, cols]
            scale = jnp.max(jnp.abs(normed), axis=1, keepdims=True) + EPS
            scale = scale.astype(BF16).astype(F32)
            quantized = (normed * (1.0 / scale)).astype(BF16).astype(F32)
            place = slice((b % per_part) * BLOCK, (b % per_part + 1) * BLOCK)
            line[h, 0, :, place] = (quantized * scale).astype(BF16)

    def route():
        lane = lax.broadcasted_iota(jnp.int32, (LANES, tokens), 0)
        named = jnp.zeros((LANES, tokens), F32)
        share = jnp.zeros((LANES, tokens), F32)
        for k in range(top):
            name = route_ref[k : k + 1, :]
            named = named + jnp.where(lane == name, 1.0, 0.0)
            share = share + jnp.where(lane - experts == name, mixing_ref[k : k + 1, :], 0.0)
        up_to = lax.broadcasted_iota(jnp.int32, (tokens, tokens), 0)
        up_to = up_to <= lax.broadcasted_iota(jnp.int32, (tokens, tokens), 1)
        place = dot(named.astype(BF16), jnp.where(up_to, 1.0, 0.0).astype(BF16))
        meta[0] = jnp.where(lane < experts, place * named, share).T.astype(BF16)

    def slots(shape, dim):
        q = lax.broadcasted_iota(jnp.int32, shape, dim)
        offset = jnp.zeros(shape, jnp.int32)
        for i in range(1, PLANE):
            offset = offset + jnp.where(q >= i * PAIR, 1, 0)
        q = q - offset * PAIR
        second = jnp.where(q >= CAPACITY, 1, 0)
        return offset, second, q - second * CAPACITY

    def owner(offset):
        dx, dy = offset >> 1, offset & 1
        return ((((mx + dx) & (NX - 1)) * NY) + ((my + dy) & (NY - 1))) * NZ + mz

    def spreads():
        offset, second, _ = slots((LANES, ROWS), 1)
        expert = owner(offset)
        lane_of = lax.broadcasted_iota(jnp.int32, (LANES, ROWS), 0)
        for i in range(2):
            for j in range(2):
                hit = (lane_of == expert + j * experts) & (second == i)
                spread[2 * j + i] = jnp.where(hit, 1.0, 0.0).astype(BF16)
        offset, second, _ = slots((ROWS, LANES), 0)
        expert = owner(offset)
        lane_of = lax.broadcasted_iota(jnp.int32, (ROWS, LANES), 1)
        for i in range(2):
            hit = (lane_of == expert) & (second == i)
            spread_t[i] = jnp.where(hit, 1.0, 0.0).astype(BF16)

    def early_pick():
        q = lax.broadcasted_iota(jnp.int32, (PLANE * EARLY, LANES), 0)
        lane_of = lax.broadcasted_iota(jnp.int32, (PLANE * EARLY, LANES), 1)
        named = jnp.where(lane_of == owner(q >> 4), 1.0, 0.0).astype(BF16)
        want = ((q & (EARLY - 1)) + 1).astype(F32)
        return jnp.where(dot_nt(named, meta[0]) == want, 1.0, 0.0).astype(BF16)

    def late_mix():
        shape = (LANES, PLANE * EARLY)
        q, lane_of = lax.broadcasted_iota(jnp.int32, shape, 1), lax.broadcasted_iota(jnp.int32, shape, 0)
        expert = owner(q >> 4)
        named = jnp.where(lane_of == expert, 1.0, 0.0).astype(BF16)
        share = jnp.where(lane_of == expert + experts, 1.0, 0.0).astype(BF16)
        q = lax.broadcasted_iota(jnp.int32, (tokens, PLANE * EARLY), 1)
        want = ((q & (EARLY - 1)) + 1).astype(F32)
        weight = dot(meta[0], share)
        mix_late[...] = jnp.where(dot(meta[0], named) == want, weight, 0.0).astype(BF16)
        for h in range(PARTS):
            lret[h, pl.ds(0, EARLY)] = jnp.zeros((EARLY, part), BF16)
            for offset in range(1, PLANE):
                ret[h, 0, pl.ds(offset * PAIR, EARLY)] = jnp.zeros((EARLY, part), BF16)

    def few(step, direction):
        if step < FAR - 1:
            return pl.ds(0, tokens)
        return pl.ds(direction * half, half)

    def gather(direction, step, h):
        source, target = ((NZ - step) % NZ, NZ - 1 - step) if direction == 0 else (step, step + 1)
        rows = few(step, direction)
        return pltpu.make_async_remote_copy(
            line.at[h, source, rows], line.at[h, target, rows],
            ag_send.at[direction, step, h], ag_recv.at[direction, step, h],
            device_id={"expert": around[direction]}, device_id_type=MESH,
        )

    def gather_meta(direction, step):
        source, target = ((NZ - step) % NZ, NZ - 1 - step) if direction == 0 else (step, step + 1)
        rows = few(step, direction)
        return pltpu.make_async_remote_copy(
            meta.at[source, rows], meta.at[target, rows],
            am_send.at[direction, step], am_recv.at[direction, step],
            device_id={"expert": around[direction]}, device_id_type=MESH,
        )

    def build(c, first, last):
        _, _, want = slots((ROWS, tokens), 0)
        want = (want + 1).astype(F32)
        for i, rel in enumerate((first, last)):
            found = dot_nt(spread_t[i], meta[rel])
            pick[:, i * tokens : (i + 1) * tokens] = jnp.where(found == want, 1.0, 0.0).astype(BF16)
        _, _, want = slots((tokens, ROWS), 1)
        want = (want + 1).astype(F32)
        for i, rel in enumerate((first, last)):
            found = dot(meta[rel], spread[i])
            weight = dot(meta[rel], spread[2 + i])
            mix[c, i * tokens : (i + 1) * tokens] = jnp.where(found == want, weight, 0.0).astype(BF16)

    def select(c, first, last, h):
        def tile(n, carry):
            cols = pl.ds(pl.multiple_of(n * TILE, TILE), TILE)
            both = jnp.concatenate([line[h, first, :, cols], line[h, last, :, cols]], axis=0)
            rows = dot(pick[...], both).astype(BF16)
            srow[h, c, :, cols] = rows
            rrow[h, c, pl.ds(0, PAIR), cols] = rows[:PAIR]
            return carry

        lax.fori_loop(0, tiles, tile, 0)

    def plane_copy(source, target, send, recv, sign, offset, c, h):
        rows = pl.ds(pl.multiple_of(offset * PAIR, 16), PAIR)
        return pltpu.make_async_remote_copy(
            source.at[h, c, rows], target.at[h, c, rows], send.at[c, h], recv.at[c, h],
            device_id={"expert": in_plane(sign, offset)}, device_id_type=MESH,
        )

    def plane_all(source, target, send, recv, c, h):
        rows = pl.ds(PAIR, ROWS - PAIR)
        return pltpu.make_async_remote_copy(
            source.at[h, c, rows], target.at[h, c, rows], send.at[c, h], recv.at[c, h],
            device_id={"expert": in_plane(1, 1)}, device_id_type=MESH,
        )

    def dispatch(c, h):
        def send(offset, carry):
            if c:
                plane_copy(srow, rrow, d_send, d_recv, 1, offset, c, h).start()
                return carry
            rows = pl.ds(pl.multiple_of(offset * PAIR + EARLY, 16), PAIR - EARLY)
            pltpu.make_async_remote_copy(
                srow.at[h, 0, rows], rrow.at[h, 0, rows], d_send.at[0, h], d_recv.at[0, h],
                device_id={"expert": in_plane(1, offset)}, device_id_type=MESH,
            ).start()
            return carry

        lax.fori_loop(1, PLANE, send, 0)

    def dispatch_early(h, chosen):
        erow[h] = dot(chosen, line[h, 0]).astype(BF16)

        def send(offset, carry):
            source = pl.ds(pl.multiple_of(offset * EARLY, 16), EARLY)
            target = pl.ds(pl.multiple_of(offset * PAIR, 16), EARLY)
            pltpu.make_async_remote_copy(
                erow.at[h, source], rrow.at[h, 0, target], d_send.at[0, h], d_recv.at[0, h],
                device_id={"expert": in_plane(1, offset)}, device_id_type=MESH,
            ).start()
            return carry

        lax.fori_loop(1, PLANE, send, 0)

    def give_back(c, h):
        def send(offset, carry):
            if c:
                plane_copy(orow, ret, r_send, r_recv, -1, offset, c, h).start()
                return carry
            rows = pl.ds(pl.multiple_of(offset * PAIR + EARLY, 16), PAIR - EARLY)
            pltpu.make_async_remote_copy(
                orow.at[h, 0, rows], ret.at[h, 0, rows], r_send.at[0, h], r_recv.at[0, h],
                device_id={"expert": in_plane(-1, offset)}, device_id_type=MESH,
            ).start()
            return carry

        lax.fori_loop(1, PLANE, send, 0)

    def late_copy(offset, h):
        source = pl.ds(pl.multiple_of(offset * PAIR, 16), EARLY)
        target = pl.ds(pl.multiple_of(offset * EARLY, 16), EARLY)
        return pltpu.make_async_remote_copy(
            orow.at[h, 0, source], lret.at[h, target], l_send.at[h], l_recv.at[h],
            device_id={"expert": in_plane(-1, offset)}, device_id_type=MESH,
        )

    def give_back_late(h):
        def send(offset, carry):
            late_copy(offset, h).start()
            return carry

        lax.fori_loop(1, PLANE, send, 0)

    def late(h):
        rows, few = pl.ds(EARLY, (PLANE - 1) * EARLY), pl.ds(PAIR, (PLANE - 1) * EARLY)
        return pltpu.make_async_remote_copy(
            orow.at[h, 0, few], lret.at[h, rows], l_send.at[h], l_recv.at[h],
            device_id={"expert": in_plane(-1, 1)}, device_id_type=MESH,
        )

    def returned(c, h):
        if c:
            return plane_all(orow, ret, r_send, r_recv, c, h)
        rows = pl.ds(PAIR, (PLANE - 1) * (PAIR - EARLY))
        return pltpu.make_async_remote_copy(
            orow.at[h, 0, rows], ret.at[h, 0, rows], r_send.at[0, h], r_recv.at[0, h],
            device_id={"expert": in_plane(-1, 1)}, device_id_type=MESH,
        )

    dispatched = functools.partial(plane_all, srow, rrow, d_send, d_recv)

    def expert_rows(c):
        for h in range(PARTS):
            dispatched(c, h).wait_recv()

        def gate(n, carry):
            total = []
            for base in (0, hidden):
                cols = pl.ds(pl.multiple_of(base + n * TILE, TILE), TILE)
                total.append(
                    sum(dot(rrow[h, c], wup[pl.ds(h * part, part), cols]) for h in range(PARTS))
                )
            g, u = total
            cols = pl.ds(pl.multiple_of(n * TILE, TILE), TILE)
            hid[:, cols] = (g / (1.0 + jnp.exp(-g)) * u).astype(BF16)
            return carry

        lax.fori_loop(0, hidden // TILE, gate, 0)

        def lower(n, carry):
            wide = pl.ds(pl.multiple_of(n * TILE, TILE), TILE)
            cols = pl.ds(pl.multiple_of((n % tiles) * TILE, TILE), TILE)
            rows = dot(hid[...], wdown[:, wide]).astype(BF16)
            orow[n // tiles, c, :, cols] = rows
            ret[n // tiles, c, pl.ds(0, PAIR), cols] = rows[:PAIR]
            return carry

        lax.fori_loop(0, PARTS * tiles, lower, 0)

    def scatter(direction, step, h):
        source = FAR - step if direction == 0 else FAR + step
        rows = pl.ds(0, tokens) if step else pl.ds(direction * half, half)
        return pltpu.make_async_remote_copy(
            rsout.at[h, source, rows], rsin.at[h, direction, step, rows],
            rs_send.at[direction, step, h], rs_recv.at[direction, step, h],
            device_id={"expert": around[direction]}, device_id_type=MESH,
        )

    def combine(c, h):
        step = FAR - c if c else 0
        returned(c, h).wait_recv()
        if step:
            for direction in range(2):
                scatter(direction, step - 1, h).wait_recv()

        def tile(n, carry):
            cols = pl.ds(pl.multiple_of(n * TILE, TILE), TILE)
            wide = pl.ds(pl.multiple_of(h * part + n * TILE, TILE), TILE)
            sums = dot(mix[c], ret[h, c, :, cols])
            near, away = sums[:tokens], sums[tokens:]
            if step == 0:
                acc[h, :, cols] = near + x_ref[:, wide].astype(F32)
                rsout[h, FAR, :, cols] = away.astype(BF16)
                return carry
            if step == 1:
                low, high = pl.ds(0, half), pl.ds(half, half)
                rsout[h, c, low, cols] = (near[:half] + rsin[h, 0, 0, low, cols].astype(F32)).astype(BF16)
                rsout[h, c, high, cols] = near[half:].astype(BF16)
                rsout[h, NZ - c, low, cols] = away[:half].astype(BF16)
                rsout[h, NZ - c, high, cols] = (away[half:] + rsin[h, 1, 0, high, cols].astype(F32)).astype(BF16)
                return carry
            rsout[h, c, :, cols] = (near + rsin[h, 0, step - 1, :, cols].astype(F32)).astype(BF16)
            rsout[h, NZ - c, :, cols] = (away + rsin[h, 1, step - 1, :, cols].astype(F32)).astype(BF16)
            return carry

        lax.fori_loop(0, tiles, tile, 0)
        for direction in range(2):
            scatter(direction, step, h).start()

    pieces = [(h, slice(0, part)) for h in range(PARTS - 1)]
    pieces += [(PARTS - 1, slice(0, part // 2)), (PARTS - 1, slice(part // 2, part))]

    def onward(i):
        h, cols = pieces[i]
        return pltpu.make_async_remote_copy(
            layer.at[h, :, cols], arrive.at[h, :, cols], sec_send.at[i], sec_recv.at[i],
            device_id={"section": following}, device_id_type=MESH,
        )

    def put(source, i):
        h, cols = pieces[i]
        place = slice(h * part + cols.start, h * part + cols.stop)
        return pltpu.make_async_copy(source.at[h, :, cols], out_ref.at[:, place], o_sem.at[i])

    route()
    load.wait()
    squares = jnp.zeros((tokens, BLOCK), F32)
    for b in range(width // BLOCK):
        values = x_ref[:, b * BLOCK : (b + 1) * BLOCK].astype(F32)
        squares = squares + values * values
    inverse = lax.rsqrt(jnp.sum(squares, axis=1, keepdims=True) / width + EPS)
    restore(0)
    pl.semaphore_wait(barrier, PLANE - 1 + 4)
    for h in range(PARTS):
        if h:
            restore(h)
        for direction in range(2):
            gather(direction, 0, h).start()
            if h == 0:
                gather_meta(direction, 0).start()
        if h == 0:
            chosen = early_pick()
        dispatch_early(h, chosen)
    for copy in weights:
        copy.start()
    spreads()
    late_mix()
    for step in range(1, FAR + 1):
        c = step % FAR
        first, last = (step, NZ - step) if c else (0, FAR)
        for direction in range(2):
            gather_meta(direction, step - 1).wait_recv()
            if c:
                gather_meta(direction, step).start()
        build(c, first, last)
        for h in range(PARTS):
            for direction in range(2):
                gather(direction, step - 1, h).wait_recv()
                if c:
                    gather(direction, step, h).start()
            select(c, first, last, h)
            dispatch(c, h)

    for copy in weights:
        copy.wait()
    for c in range(1, FAR):
        expert_rows(c)
    for h in range(PARTS):
        give_back(FAR - 1, h)
    expert_rows(0)
    for h in range(PARTS):
        give_back(0, h)
    for c in range(FAR - 2, 0, -1):
        for h in range(PARTS):
            give_back(c, h)
    for h in range(PARTS):
        give_back_late(h)
    for c in (0, *range(FAR - 1, 0, -1)):
        for h in range(PARTS):
            combine(c, h)
    for i, (h, cols) in enumerate(pieces):
        if cols.start == 0:
            for direction in range(2):
                scatter(direction, FAR - 1, h).wait_recv()
            late(h).wait_recv()
        total = acc[h, :, cols] + rsin[h, 0, FAR - 1, :, cols].astype(F32)
        total = total + rsin[h, 1, FAR - 1, :, cols].astype(F32)
        total = total + dot(mix_late[...], lret[h, :, cols])
        layer[h, :, cols] = total.astype(BF16)
        onward(i).start()

    @pl.when(section != 0)
    def _():
        for i in range(len(pieces)):
            onward(i).wait_recv()
            put(arrive, i).start()
        for i in range(len(pieces)):
            put(arrive, i).wait()

    @pl.when(section == 0)
    def _():
        squares = jnp.zeros((tokens, BLOCK), F32)
        for i, (h, cols) in enumerate(pieces):
            onward(i).wait_recv()
            for place in range(cols.start, cols.stop, BLOCK):
                values = arrive[h, :, place : place + BLOCK].astype(F32)
                squares = squares + values * values
        inverse = lax.rsqrt(jnp.sum(squares, axis=1, keepdims=True) / width + EPS)
        for i, (h, cols) in enumerate(pieces):
            for place in range(cols.start, cols.stop, BLOCK):
                values = arrive[h, :, place : place + BLOCK].astype(F32)
                gain = final_ref[:, h * part + place : h * part + place + BLOCK]
                normed[h, :, place : place + BLOCK] = (values * inverse * gain).astype(BF16)
            put(normed, i).start()
        for i in range(len(pieces)):
            put(normed, i).wait()

    for h in range(PARTS):
        for step in range(FAR):
            for direction in range(2):
                gather(direction, step, h).wait_send()
                scatter(direction, step, h).wait_send()
        for c in range(FAR):
            dispatched(c, h).wait_send()
            returned(c, h).wait_send()
        late(h).wait_send()
    for i in range(len(pieces)):
        onward(i).wait_send()
    for step in range(FAR):
        for direction in range(2):
            gather_meta(direction, step).wait_send()


def local(pending, gain, final_gain, assigned, mixing, raising, lowering):
    x = pending[0]
    tokens, width = x.shape
    hidden = lowering.shape[2]
    part = width // PARTS
    vmem = pl.BlockSpec(memory_space=pltpu.VMEM)
    hbm = pl.BlockSpec(memory_space=pl.ANY)
    sems = pltpu.SemaphoreType.DMA
    arrived = pl.pallas_call(
        body,
        out_shape=jax.ShapeDtypeStruct((tokens, width), BF16),
        in_specs=[hbm, vmem, vmem, vmem, vmem, hbm, hbm],
        out_specs=hbm,
        scratch_shapes=[
            pltpu.VMEM((tokens, width), BF16),
            pltpu.VMEM((PARTS, NZ, tokens, part), BF16),
            pltpu.VMEM((NZ, tokens, LANES), BF16),
            pltpu.VMEM((PARTS, FAR, ROWS, part), BF16),
            pltpu.VMEM((PARTS, FAR, ROWS, part), BF16),
            pltpu.VMEM((PARTS, FAR, ROWS, part), BF16),
            pltpu.VMEM((PARTS, FAR, ROWS, part), BF16),
            pltpu.VMEM((PARTS, PLANE * EARLY, part), BF16),
            pltpu.VMEM((PARTS, PLANE * EARLY, part), BF16),
            pltpu.VMEM((FAR, 2 * tokens, ROWS), BF16),
            pltpu.VMEM((tokens, PLANE * EARLY), BF16),
            pltpu.VMEM((ROWS, 2 * tokens), BF16),
            pltpu.VMEM((4, LANES, ROWS), BF16),
            pltpu.VMEM((2, ROWS, LANES), BF16),
            pltpu.VMEM((width, 2 * hidden), BF16),
            pltpu.VMEM((hidden, width), BF16),
            pltpu.VMEM((ROWS, hidden), BF16),
            pltpu.VMEM((PARTS, tokens, part), F32),
            pltpu.VMEM((PARTS, NZ, tokens, part), BF16),
            pltpu.VMEM((PARTS, 2, FAR, tokens, part), BF16),
            pltpu.VMEM((PARTS, tokens, part), BF16),
            pltpu.VMEM((PARTS, tokens, part), BF16),
            pltpu.VMEM((PARTS, tokens, part), BF16),
            sems((2, FAR, PARTS)),
            sems((2, FAR, PARTS)),
            sems((2, FAR)),
            sems((2, FAR)),
            sems((FAR, PARTS)),
            sems((FAR, PARTS)),
            sems((FAR, PARTS)),
            sems((FAR, PARTS)),
            sems((2, FAR, PARTS)),
            sems((2, FAR, PARTS)),
            sems((PARTS + 1,)),
            sems((PARTS + 1,)),
            sems((PARTS,)),
            sems((PARTS,)),
            sems((PARTS + 1,)),
            sems((3,)),
        ],
        compiler_params=pltpu.CompilerParams(
            collective_id=0, has_side_effects=True, vmem_limit_bytes=62 << 20
        ),
        name="relay_step",
    )(x, gain, final_gain[None], assigned[0].T, mixing[0].T, raising[0, 0], lowering[0, 0])
    return arrived[None]


def solution(mesh):
    in_specs = (
        P("section", "expert", None),
        P("section", None),
        P(),
        P("section", "expert", None),
        P("section", "expert", None),
        P("section", "expert", None, None),
        P("section", "expert", None, None),
    )
    out_specs = P("section", "expert", None)
    return jax.shard_map(local, mesh=mesh, in_specs=in_specs, out_specs=out_specs, check_vma=False)
```

```python
import functools

import jax
import jax.numpy as jnp
from jax import lax
from jax.experimental import pallas as pl
from jax.experimental.pallas import tpu as pltpu
from jax.sharding import PartitionSpec as P

MESH = pl.DeviceIdType.MESH
F32, BF16 = jnp.float32, jnp.bfloat16
BLOCK = 128
EPS = 1e-06
NX, NY, NZ = 4, 2, 8
PLANE = NX * NY
FAR = NZ // 2
CAPACITY = 24
PAIR = 2 * CAPACITY
ROWS = PLANE * PAIR
PARTS = 4
TILE = 256
EARLY = 16
LANES = 128


def dot(a, b):
    return jnp.dot(a, b, preferred_element_type=F32)


def dot_nt(a, b):
    return lax.dot_general(a, b, (((1,), (1,)), ((), ())), preferred_element_type=F32)


def body(
    x_hbm, gain_ref, final_ref, route_ref, mixing_ref, up_ref, down_ref, out_ref,
    x_ref, line, meta, srow, rrow, orow, ret, erow, lret, mix, mix_late, pick, spread, spread_t, wup, wdown, hid,
    acc, rsout, rsin, layer, arrive, normed,
    ag_send, ag_recv, am_send, am_recv, d_send, d_recv, r_send, r_recv,
    rs_send, rs_recv, sec_send, sec_recv, l_send, l_recv, o_sem, w_sem,
):
    tokens, width = x_ref.shape
    part = width // PARTS
    hidden = wdown.shape[0]
    top = route_ref.shape[0]
    per_part = part // BLOCK
    tiles = part // TILE
    experts = PLANE * NZ
    half = tokens // 2
    me = lax.axis_index("expert")
    section = lax.axis_index("section")
    sections = lax.axis_size("section")
    mx, my, mz = me // (NY * NZ), (me // NZ) % NY, me % NZ

    def in_plane(sign, offset):
        dx, dy = offset // NY, offset % NY
        return (((mx + sign * dx + NX) % NX) * NY + (my + dy) % NY) * NZ + mz

    column = me - mz
    around = (column + (mz + 1) % NZ, column + (mz + NZ - 1) % NZ)
    following = (section + 1) % sections
    previous = (section + sections - 1) % sections

    load = pltpu.make_async_copy(x_hbm, x_ref, w_sem.at[2])
    load.start()
    weights = [
        pltpu.make_async_copy(up_ref, wup, w_sem.at[0]),
        pltpu.make_async_copy(down_ref, wdown, w_sem.at[1]),
    ]

    barrier = pltpu.get_barrier_semaphore()

    def greet(offset, carry):
        pl.semaphore_signal(
            barrier, 1, device_id={"expert": in_plane(1, offset)}, device_id_type=MESH
        )
        return carry

    lax.fori_loop(1, PLANE, greet, 0)
    for peer in around:
        pl.semaphore_signal(barrier, 1, device_id={"expert": peer}, device_id_type=MESH)
    for peer in (following, previous):
        pl.semaphore_signal(barrier, 1, device_id={"section": peer}, device_id_type=MESH)

    def restore(h):
        for b in range(h * per_part, (h + 1) * per_part):
            cols = slice(b * BLOCK, (b + 1) * BLOCK)
            normed = x_ref[:, cols].astype(F32) * inverse * gain_ref[:, cols]
            scale = jnp.max(jnp.abs(normed), axis=1, keepdims=True) + EPS
            scale = scale.astype(BF16).astype(F32)
            quantized = (normed * (1.0 / scale)).astype(BF16).astype(F32)
            place = slice((b % per_part) * BLOCK, (b % per_part + 1) * BLOCK)
            line[h, 0, :, place] = (quantized * scale).astype(BF16)

    def route():
        lane = lax.broadcasted_iota(jnp.int32, (LANES, tokens), 0)
        named = jnp.zeros((LANES, tokens), F32)
        share = jnp.zeros((LANES, tokens), F32)
        for k in range(top):
            name = route_ref[k : k + 1, :]
            named = named + jnp.where(lane == name, 1.0, 0.0)
            share = share + jnp.where(lane - experts == name, mixing_ref[k : k + 1, :], 0.0)
        up_to = lax.broadcasted_iota(jnp.int32, (tokens, tokens), 0)
        up_to = up_to <= lax.broadcasted_iota(jnp.int32, (tokens, tokens), 1)
        place = dot(named.astype(BF16), jnp.where(up_to, 1.0, 0.0).astype(BF16))
        meta[0] = jnp.where(lane < experts, place * named, share).T.astype(BF16)

    def slots(shape, dim):
        q = lax.broadcasted_iota(jnp.int32, shape, dim)
        offset = jnp.zeros(shape, jnp.int32)
        for i in range(1, PLANE):
            offset = offset + jnp.where(q >= i * PAIR, 1, 0)
        q = q - offset * PAIR
        second = jnp.where(q >= CAPACITY, 1, 0)
        return offset, second, q - second * CAPACITY

    def owner(offset):
        dx, dy = offset >> 1, offset & 1
        return ((((mx + dx) & (NX - 1)) * NY) + ((my + dy) & (NY - 1))) * NZ + mz

    def spreads():
        offset, second, _ = slots((LANES, ROWS), 1)
        expert = owner(offset)
        lane_of = lax.broadcasted_iota(jnp.int32, (LANES, ROWS), 0)
        for i in range(2):
            for j in range(2):
                hit = (lane_of == expert + j * experts) & (second == i)
                spread[2 * j + i] = jnp.where(hit, 1.0, 0.0).astype(BF16)
        offset, second, _ = slots((ROWS, LANES), 0)
        expert = owner(offset)
        lane_of = lax.broadcasted_iota(jnp.int32, (ROWS, LANES), 1)
        for i in range(2):
            hit = (lane_of == expert) & (second == i)
            spread_t[i] = jnp.where(hit, 1.0, 0.0).astype(BF16)

    def early_pick():
        q = lax.broadcasted_iota(jnp.int32, (PLANE * EARLY, LANES), 0)
        lane_of = lax.broadcasted_iota(jnp.int32, (PLANE * EARLY, LANES), 1)
        named = jnp.where(lane_of == owner(q >> 4), 1.0, 0.0).astype(BF16)
        want = ((q & (EARLY - 1)) + 1).astype(F32)
        return jnp.where(dot_nt(named, meta[0]) == want, 1.0, 0.0).astype(BF16)

    def late_mix():
        shape = (LANES, PLANE * EARLY)
        q, lane_of = lax.broadcasted_iota(jnp.int32, shape, 1), lax.broadcasted_iota(jnp.int32, shape, 0)
        expert = owner(q >> 4)
        named = jnp.where(lane_of == expert, 1.0, 0.0).astype(BF16)
        share = jnp.where(lane_of == expert + experts, 1.0, 0.0).astype(BF16)
        q = lax.broadcasted_iota(jnp.int32, (tokens, PLANE * EARLY), 1)
        want = ((q & (EARLY - 1)) + 1).astype(F32)
        weight = dot(meta[0], share)
        mix_late[...] = jnp.where(dot(meta[0], named) == want, weight, 0.0).astype(BF16)
        for h in range(PARTS):
            lret[h, pl.ds(0, EARLY)] = jnp.zeros((EARLY, part), BF16)
            for offset in range(1, PLANE):
                ret[h, 0, pl.ds(offset * PAIR, EARLY)] = jnp.zeros((EARLY, part), BF16)

    def few(step, direction):
        if step < FAR - 1:
            return pl.ds(0, tokens)
        return pl.ds(direction * half, half)

    def gather(direction, step, h):
        source, target = ((NZ - step) % NZ, NZ - 1 - step) if direction == 0 else (step, step + 1)
        rows = few(step, direction)
        return pltpu.make_async_remote_copy(
            line.at[h, source, rows], line.at[h, target, rows],
            ag_send.at[direction, step, h], ag_recv.at[direction, step, h],
            device_id={"expert": around[direction]}, device_id_type=MESH,
        )

    def gather_meta(direction, step):
        source, target = ((NZ - step) % NZ, NZ - 1 - step) if direction == 0 else (step, step + 1)
        rows = few(step, direction)
        return pltpu.make_async_remote_copy(
            meta.at[source, rows], meta.at[target, rows],
            am_send.at[direction, step], am_recv.at[direction, step],
            device_id={"expert": around[direction]}, device_id_type=MESH,
        )

    def build(c, first, last):
        _, _, want = slots((ROWS, tokens), 0)
        want = (want + 1).astype(F32)
        for i, rel in enumerate((first, last)):
            found = dot_nt(spread_t[i], meta[rel])
            pick[:, i * tokens : (i + 1) * tokens] = jnp.where(found == want, 1.0, 0.0).astype(BF16)
        _, _, want = slots((tokens, ROWS), 1)
        want = (want + 1).astype(F32)
        for i, rel in enumerate((first, last)):
            found = dot(meta[rel], spread[i])
            weight = dot(meta[rel], spread[2 + i])
            mix[c, i * tokens : (i + 1) * tokens] = jnp.where(found == want, weight, 0.0).astype(BF16)

    def select(c, first, last, h):
        def tile(n, carry):
            cols = pl.ds(pl.multiple_of(n * TILE, TILE), TILE)
            both = jnp.concatenate([line[h, first, :, cols], line[h, last, :, cols]], axis=0)
            rows = dot(pick[...], both).astype(BF16)
            srow[h, c, :, cols] = rows
            rrow[h, c, pl.ds(0, PAIR), cols] = rows[:PAIR]
            return carry

        lax.fori_loop(0, tiles, tile, 0)

    def plane_copy(source, target, send, recv, sign, offset, c, h):
        rows = pl.ds(pl.multiple_of(offset * PAIR, 16), PAIR)
        return pltpu.make_async_remote_copy(
            source.at[h, c, rows], target.at[h, c, rows], send.at[c, h], recv.at[c, h],
            device_id={"expert": in_plane(sign, offset)}, device_id_type=MESH,
        )

    def plane_all(source, target, send, recv, c, h):
        rows = pl.ds(PAIR, ROWS - PAIR)
        return pltpu.make_async_remote_copy(
            source.at[h, c, rows], target.at[h, c, rows], send.at[c, h], recv.at[c, h],
            device_id={"expert": in_plane(1, 1)}, device_id_type=MESH,
        )

    def dispatch(c, h):
        def send(offset, carry):
            if c:
                plane_copy(srow, rrow, d_send, d_recv, 1, offset, c, h).start()
                return carry
            rows = pl.ds(pl.multiple_of(offset * PAIR + EARLY, 16), PAIR - EARLY)
            pltpu.make_async_remote_copy(
                srow.at[h, 0, rows], rrow.at[h, 0, rows], d_send.at[0, h], d_recv.at[0, h],
                device_id={"expert": in_plane(1, offset)}, device_id_type=MESH,
            ).start()
            return carry

        lax.fori_loop(1, PLANE, send, 0)

    def dispatch_early(h, chosen):
        erow[h] = dot(chosen, line[h, 0]).astype(BF16)

        def send(offset, carry):
            source = pl.ds(pl.multiple_of(offset * EARLY, 16), EARLY)
            target = pl.ds(pl.multiple_of(offset * PAIR, 16), EARLY)
            pltpu.make_async_remote_copy(
                erow.at[h, source], rrow.at[h, 0, target], d_send.at[0, h], d_recv.at[0, h],
                device_id={"expert": in_plane(1, offset)}, device_id_type=MESH,
            ).start()
            return carry

        lax.fori_loop(1, PLANE, send, 0)

    def give_back(c, h):
        def send(offset, carry):
            if c:
                plane_copy(orow, ret, r_send, r_recv, -1, offset, c, h).start()
                return carry
            rows = pl.ds(pl.multiple_of(offset * PAIR + EARLY, 16), PAIR - EARLY)
            pltpu.make_async_remote_copy(
                orow.at[h, 0, rows], ret.at[h, 0, rows], r_send.at[0, h], r_recv.at[0, h],
                device_id={"expert": in_plane(-1, offset)}, device_id_type=MESH,
            ).start()
            return carry

        lax.fori_loop(1, PLANE, send, 0)

    def late_copy(offset, h):
        source = pl.ds(pl.multiple_of(offset * PAIR, 16), EARLY)
        target = pl.ds(pl.multiple_of(offset * EARLY, 16), EARLY)
        return pltpu.make_async_remote_copy(
            orow.at[h, 0, source], lret.at[h, target], l_send.at[h], l_recv.at[h],
            device_id={"expert": in_plane(-1, offset)}, device_id_type=MESH,
        )

    def give_back_late(h):
        def send(offset, carry):
            late_copy(offset, h).start()
            return carry

        lax.fori_loop(1, PLANE, send, 0)

    def late(h):
        rows, few = pl.ds(EARLY, (PLANE - 1) * EARLY), pl.ds(PAIR, (PLANE - 1) * EARLY)
        return pltpu.make_async_remote_copy(
            orow.at[h, 0, few], lret.at[h, rows], l_send.at[h], l_recv.at[h],
            device_id={"expert": in_plane(-1, 1)}, device_id_type=MESH,
        )

    def returned(c, h):
        if c:
            return plane_all(orow, ret, r_send, r_recv, c, h)
        rows = pl.ds(PAIR, (PLANE - 1) * (PAIR - EARLY))
        return pltpu.make_async_remote_copy(
            orow.at[h, 0, rows], ret.at[h, 0, rows], r_send.at[0, h], r_recv.at[0, h],
            device_id={"expert": in_plane(-1, 1)}, device_id_type=MESH,
        )

    dispatched = functools.partial(plane_all, srow, rrow, d_send, d_recv)

    def expert_rows(c):
        for h in range(PARTS):
            dispatched(c, h).wait_recv()

        def gate(n, carry):
            total = []
            for base in (0, hidden):
                cols = pl.ds(pl.multiple_of(base + n * TILE, TILE), TILE)
                total.append(
                    sum(dot(rrow[h, c], wup[pl.ds(h * part, part), cols]) for h in range(PARTS))
                )
            g, u = total
            cols = pl.ds(pl.multiple_of(n * TILE, TILE), TILE)
            hid[:, cols] = (g / (1.0 + jnp.exp(-g)) * u).astype(BF16)
            return carry

        lax.fori_loop(0, hidden // TILE, gate, 0)

        for h in range(PARTS):

            def lower(n, carry):
                cols = pl.ds(pl.multiple_of(n * TILE, TILE), TILE)
                wide = pl.ds(pl.multiple_of(h * part + n * TILE, TILE), TILE)
                rows = dot(hid[...], wdown[:, wide]).astype(BF16)
                orow[h, c, :, cols] = rows
                ret[h, c, pl.ds(0, PAIR), cols] = rows[:PAIR]
                return carry

            lax.fori_loop(0, tiles, lower, 0)
            if c in (0, FAR - 1):
                give_back(c, h)

    def scatter(direction, step, h):
        source = FAR - step if direction == 0 else FAR + step
        rows = pl.ds(0, tokens) if step else pl.ds(direction * half, half)
        return pltpu.make_async_remote_copy(
            rsout.at[h, source, rows], rsin.at[h, direction, step, rows],
            rs_send.at[direction, step, h], rs_recv.at[direction, step, h],
            device_id={"expert": around[direction]}, device_id_type=MESH,
        )

    def combine(c, h):
        step = FAR - c if c else 0
        returned(c, h).wait_recv()
        if step:
            for direction in range(2):
                scatter(direction, step - 1, h).wait_recv()

        def tile(n, carry):
            cols = pl.ds(pl.multiple_of(n * TILE, TILE), TILE)
            wide = pl.ds(pl.multiple_of(h * part + n * TILE, TILE), TILE)
            sums = dot(mix[c], ret[h, c, :, cols])
            near, away = sums[:tokens], sums[tokens:]
            if step == 0:
                acc[h, :, cols] = near + x_ref[:, wide].astype(F32)
                rsout[h, FAR, :, cols] = away.astype(BF16)
                return carry
            if step == 1:
                low, high = pl.ds(0, half), pl.ds(half, half)
                rsout[h, c, low, cols] = (near[:half] + rsin[h, 0, 0, low, cols].astype(F32)).astype(BF16)
                rsout[h, c, high, cols] = near[half:].astype(BF16)
                rsout[h, NZ - c, low, cols] = away[:half].astype(BF16)
                rsout[h, NZ - c, high, cols] = (away[half:] + rsin[h, 1, 0, high, cols].astype(F32)).astype(BF16)
                return carry
            rsout[h, c, :, cols] = (near + rsin[h, 0, step - 1, :, cols].astype(F32)).astype(BF16)
            rsout[h, NZ - c, :, cols] = (away + rsin[h, 1, step - 1, :, cols].astype(F32)).astype(BF16)
            return carry

        lax.fori_loop(0, tiles, tile, 0)
        for direction in range(2):
            scatter(direction, step, h).start()

    pieces = [(h, slice(0, part)) for h in range(PARTS - 1)]
    pieces += [(PARTS - 1, slice(0, part // 2)), (PARTS - 1, slice(part // 2, part))]

    def onward(i):
        h, cols = pieces[i]
        return pltpu.make_async_remote_copy(
            layer.at[h, :, cols], arrive.at[h, :, cols], sec_send.at[i], sec_recv.at[i],
            device_id={"section": following}, device_id_type=MESH,
        )

    def put(source, i):
        h, cols = pieces[i]
        place = slice(h * part + cols.start, h * part + cols.stop)
        return pltpu.make_async_copy(source.at[h, :, cols], out_ref.at[:, place], o_sem.at[i])

    route()
    load.wait()
    squares = jnp.zeros((tokens, BLOCK), F32)
    for b in range(width // BLOCK):
        values = x_ref[:, b * BLOCK : (b + 1) * BLOCK].astype(F32)
        squares = squares + values * values
    inverse = lax.rsqrt(jnp.sum(squares, axis=1, keepdims=True) / width + EPS)
    restore(0)
    pl.semaphore_wait(barrier, PLANE - 1 + 4)
    for h in range(PARTS):
        if h:
            restore(h)
        for direction in range(2):
            gather(direction, 0, h).start()
            if h == 0:
                gather_meta(direction, 0).start()
        if h == 0:
            chosen = early_pick()
        dispatch_early(h, chosen)
    for copy in weights:
        copy.start()
    spreads()
    late_mix()
    for step in range(1, FAR + 1):
        c = step % FAR
        first, last = (step, NZ - step) if c else (0, FAR)
        for direction in range(2):
            gather_meta(direction, step - 1).wait_recv()
            if c:
                gather_meta(direction, step).start()
        build(c, first, last)
        for h in range(PARTS):
            for direction in range(2):
                gather(direction, step - 1, h).wait_recv()
                if c:
                    gather(direction, step, h).start()
            select(c, first, last, h)
            dispatch(c, h)

    for copy in weights:
        copy.wait()
    for c in range(1, FAR):
        expert_rows(c)
    expert_rows(0)
    for c in range(FAR - 2, 0, -1):
        for h in range(PARTS):
            give_back(c, h)
    for h in range(PARTS):
        give_back_late(h)
    for c in (0, *range(FAR - 1, 0, -1)):
        for h in range(PARTS):
            combine(c, h)
    for i, (h, cols) in enumerate(pieces):
        if cols.start == 0:
            for direction in range(2):
                scatter(direction, FAR - 1, h).wait_recv()
            late(h).wait_recv()
        total = acc[h, :, cols] + rsin[h, 0, FAR - 1, :, cols].astype(F32)
        total = total + rsin[h, 1, FAR - 1, :, cols].astype(F32)
        total = total + dot(mix_late[...], lret[h, :, cols])
        layer[h, :, cols] = total.astype(BF16)
        onward(i).start()

    @pl.when(section != 0)
    def _():
        for i in range(len(pieces)):
            onward(i).wait_recv()
            put(arrive, i).start()
        for i in range(len(pieces)):
            put(arrive, i).wait()

    @pl.when(section == 0)
    def _():
        squares = jnp.zeros((tokens, BLOCK), F32)
        for i, (h, cols) in enumerate(pieces):
            onward(i).wait_recv()
            for place in range(cols.start, cols.stop, BLOCK):
                values = arrive[h, :, place : place + BLOCK].astype(F32)
                squares = squares + values * values
        inverse = lax.rsqrt(jnp.sum(squares, axis=1, keepdims=True) / width + EPS)
        for i, (h, cols) in enumerate(pieces):
            for place in range(cols.start, cols.stop, BLOCK):
                values = arrive[h, :, place : place + BLOCK].astype(F32)
                gain = final_ref[:, h * part + place : h * part + place + BLOCK]
                normed[h, :, place : place + BLOCK] = (values * inverse * gain).astype(BF16)
            put(normed, i).start()
        for i in range(len(pieces)):
            put(normed, i).wait()

    for h in range(PARTS):
        for step in range(FAR):
            for direction in range(2):
                gather(direction, step, h).wait_send()
                scatter(direction, step, h).wait_send()
        for c in range(FAR):
            dispatched(c, h).wait_send()
            returned(c, h).wait_send()
        late(h).wait_send()
    for i in range(len(pieces)):
        onward(i).wait_send()
    for step in range(FAR):
        for direction in range(2):
            gather_meta(direction, step).wait_send()


def local(pending, gain, final_gain, assigned, mixing, raising, lowering):
    x = pending[0]
    tokens, width = x.shape
    hidden = lowering.shape[2]
    part = width // PARTS
    vmem = pl.BlockSpec(memory_space=pltpu.VMEM)
    hbm = pl.BlockSpec(memory_space=pl.ANY)
    sems = pltpu.SemaphoreType.DMA
    arrived = pl.pallas_call(
        body,
        out_shape=jax.ShapeDtypeStruct((tokens, width), BF16),
        in_specs=[hbm, vmem, vmem, vmem, vmem, hbm, hbm],
        out_specs=hbm,
        scratch_shapes=[
            pltpu.VMEM((tokens, width), BF16),
            pltpu.VMEM((PARTS, NZ, tokens, part), BF16),
            pltpu.VMEM((NZ, tokens, LANES), BF16),
            pltpu.VMEM((PARTS, FAR, ROWS, part), BF16),
            pltpu.VMEM((PARTS, FAR, ROWS, part), BF16),
            pltpu.VMEM((PARTS, FAR, ROWS, part), BF16),
            pltpu.VMEM((PARTS, FAR, ROWS, part), BF16),
            pltpu.VMEM((PARTS, PLANE * EARLY, part), BF16),
            pltpu.VMEM((PARTS, PLANE * EARLY, part), BF16),
            pltpu.VMEM((FAR, 2 * tokens, ROWS), BF16),
            pltpu.VMEM((tokens, PLANE * EARLY), BF16),
            pltpu.VMEM((ROWS, 2 * tokens), BF16),
            pltpu.VMEM((4, LANES, ROWS), BF16),
            pltpu.VMEM((2, ROWS, LANES), BF16),
            pltpu.VMEM((width, 2 * hidden), BF16),
            pltpu.VMEM((hidden, width), BF16),
            pltpu.VMEM((ROWS, hidden), BF16),
            pltpu.VMEM((PARTS, tokens, part), F32),
            pltpu.VMEM((PARTS, NZ, tokens, part), BF16),
            pltpu.VMEM((PARTS, 2, FAR, tokens, part), BF16),
            pltpu.VMEM((PARTS, tokens, part), BF16),
            pltpu.VMEM((PARTS, tokens, part), BF16),
            pltpu.VMEM((PARTS, tokens, part), BF16),
            sems((2, FAR, PARTS)),
            sems((2, FAR, PARTS)),
            sems((2, FAR)),
            sems((2, FAR)),
            sems((FAR, PARTS)),
            sems((FAR, PARTS)),
            sems((FAR, PARTS)),
            sems((FAR, PARTS)),
            sems((2, FAR, PARTS)),
            sems((2, FAR, PARTS)),
            sems((PARTS + 1,)),
            sems((PARTS + 1,)),
            sems((PARTS,)),
            sems((PARTS,)),
            sems((PARTS + 1,)),
            sems((3,)),
        ],
        compiler_params=pltpu.CompilerParams(
            collective_id=0, has_side_effects=True, vmem_limit_bytes=62 << 20
        ),
        name="relay_step",
    )(x, gain, final_gain[None], assigned[0].T, mixing[0].T, raising[0, 0], lowering[0, 0])
    return arrived[None]


def solution(mesh):
    in_specs = (
        P("section", "expert", None),
        P("section", None),
        P(),
        P("section", "expert", None),
        P("section", "expert", None),
        P("section", "expert", None, None),
        P("section", "expert", None, None),
    )
    out_specs = P("section", "expert", None)
    return jax.shard_map(local, mesh=mesh, in_specs=in_specs, out_specs=out_specs, check_vma=False)
```
